256 devices in a mesh: blk: 16 (over z, y_lo), rep: 16 (over y_hi, x, core).
Axes of the slice: x: 4, y: 4 (y_hi: 2, y_lo: 2; y = y_hi * 2 + y_lo), z: 8, core: 2. Of those that a mesh axis runs over, the one named last changes fastest.
Arguments:
- image_feats: bfloat16 [16, 2048, 1152], P('rep', 'blk'), may hold values from -7 to 7
- text_feats: bfloat16 [16, 2048, 1152], P('rep', 'blk'), may hold values from -7 to 7
- image_head: bfloat16 [1152, 1152], replicated, may hold values from -0.1875 to 0.1875
- text_head: bfloat16 [1152, 1152], replicated, may hold values from -0.1875 to 0.1875
- log_scale: float32 [1], replicated, may hold values from 1.4 to 2.8
- bias: float32 [1], replicated, may hold values from -4 to -2
Outputs:
- grad_image_feats: bfloat16 [16, 2048, 1152], P('rep', 'blk')
- grad_text_feats: bfloat16 [16, 2048, 1152], P('rep', 'blk')
- head_grads: float32 [1152, 2, 1152], P('blk')
The draws below stay inside these ranges and needn't reach their ends.
All inputs are finite; a program needn't handle non-finite values.
Results may differ from the reference program's by a relative error of at most 0.02.
Values may be sent and summed in bfloat16 or wider, within the bound.
No kernel may reach another device: no remote copies, remote signals or barrier semaphores. Data moves between devices by JAX's collectives and lax.ppermute only.
A program may use at most 128 MiB of HBM per device.

```python
import jax
import jax.numpy as jnp
from jax import lax

D = 1152
ROWS = 128
STEPS = 4
BATCH = 2048
REPLICAS = 16
N_BLK = 16


def draw_image_feats(key, part):
    key = jax.random.fold_in(key, 11)
    key_rows, key_cols, key_vals = jax.random.split(key, 3)
    shape = (REPLICAS, BATCH, D)
    row_scale = jnp.exp(2.302585 * jax.random.uniform(key_rows, (REPLICAS, BATCH, 1), jnp.float32, -0.5, 0.5))
    col_scale = jnp.exp(2.302585 * jax.random.uniform(key_cols, (1, 1, D), jnp.float32, -0.5, 0.5))
    values = jnp.clip(jax.random.normal(key_vals, shape, jnp.float32), -4.0, 4.0)
    return (0.1 * row_scale * col_scale * values).astype(jnp.bfloat16)


def draw_text_feats(key, part):
    key = jax.random.fold_in(key, 12)
    key_rows, key_cols, key_vals = jax.random.split(key, 3)
    shape = (REPLICAS, BATCH, D)
    row_scale = jnp.exp(2.302585 * jax.random.uniform(key_rows, (REPLICAS, BATCH, 1), jnp.float32, -0.5, 0.5))
    col_scale = jnp.exp(2.302585 * jax.random.uniform(key_cols, (1, 1, D), jnp.float32, -0.5, 0.5))
    values = jnp.clip(jax.random.normal(key_vals, shape, jnp.float32), -4.0, 4.0)
    return (0.1 * row_scale * col_scale * values).astype(jnp.bfloat16)


def gaussian(rng, dims, spread, limit, held_as=jnp.bfloat16):
    array = jax.random.normal(rng, dims, jnp.float32) * spread
    return jnp.minimum(jnp.maximum(array, -limit), limit).astype(held_as)


def setup_inputs(seed: int = 0) -> dict:
    keys = jax.random.split(jax.random.key(seed), 7)
    return {
        "image_feats": draw_image_feats(jax.random.fold_in(keys[6], 71), 0),
        "text_feats": draw_text_feats(jax.random.fold_in(keys[6], 71), 0),
        "image_head": gaussian(keys[2], (D, D), D ** -0.5, 0.1875),
        "text_head": gaussian(keys[3], (D, D), D ** -0.5, 0.1875),
        "log_scale": jnp.clip(jax.random.uniform(keys[4], (1,), jnp.float32, 1.4, 2.8), 1.4, 2.8),
        "bias": jnp.clip(jax.random.uniform(keys[5], (1,), jnp.float32, -4.0, -2.0), -4.0, -2.0),
    }


EPSILON = 1e-06

def project_rows(features, head):
    projected = jnp.dot(features, head, preferred_element_type=jnp.float32)
    row_norm = jnp.sqrt(lax.optimization_barrier(jnp.sum(projected * projected, axis=1, keepdims=True)) + EPSILON)
    return (projected / row_norm, row_norm)

def unit_backward(unit_grad, unit_rows, row_norm):
    radial = lax.optimization_barrier(jnp.sum(unit_rows * unit_grad, axis=1, keepdims=True))
    return ((unit_grad - unit_rows * radial) / row_norm).astype(jnp.bfloat16)

def contract_rows(left, right):
    return lax.dot_general(left, right, (((0,), (0,)), ((), ())), preferred_element_type=jnp.float32)

def contract_cols(left, right):
    return lax.dot_general(left, right, (((1,), (1,)), ((), ())), preferred_element_type=jnp.float32)

def reference(image_feats, text_feats, image_head, text_head, log_scale, bias):
    logit_scale = jnp.exp(log_scale[0])
    offset = bias[0]
    positives = jnp.eye(ROWS, dtype=jnp.float32)

    def one_replica(totals, pair):
        image_rows, text_rows = pair
        image_unit, image_norm = project_rows(image_rows, image_head)
        text_unit, text_norm = project_rows(text_rows, text_head)
        image_emb = lax.optimization_barrier(image_unit.astype(jnp.bfloat16)).astype(jnp.float32).reshape(N_BLK, ROWS, D)
        text_emb = lax.optimization_barrier(text_unit.astype(jnp.bfloat16)).astype(jnp.float32).reshape(N_BLK, ROWS, D)
        image_grad = jnp.zeros((N_BLK, ROWS, D), jnp.float32)
        text_grad = jnp.zeros((N_BLK, ROWS, D), jnp.float32)
        for turn_index in range(STEPS):
            visiting = jnp.roll(text_emb, turn_index, axis=0)
            logits = logit_scale * jnp.einsum('bid,bjd->bij', image_emb, visiting) + offset
            probs = jax.nn.sigmoid(logits)
            if turn_index == 0:
                probs = probs - positives
            weights = lax.optimization_barrier((logit_scale * probs).astype(jnp.bfloat16)).astype(jnp.float32)
            image_grad = image_grad + jnp.einsum('bij,bjd->bid', weights, visiting)
            text_part = jnp.einsum('bij,bid->bjd', weights, image_emb)
            text_grad = text_grad + jnp.roll(text_part, -turn_index, axis=0)
        image_dpre = unit_backward(image_grad.reshape(BATCH, D), image_unit, image_norm)
        text_dpre = unit_backward(text_grad.reshape(BATCH, D), text_unit, text_norm)
        image_out = contract_cols(image_dpre, image_head).astype(jnp.bfloat16)
        text_out = contract_cols(text_dpre, text_head).astype(jnp.bfloat16)
        totals = (totals[0] + contract_rows(image_rows, image_dpre), totals[1] + contract_rows(text_rows, text_dpre))
        return (totals, (image_out, text_out))
    zero_sum = jnp.zeros((D, D), jnp.float32)
    totals, outputs = lax.scan(one_replica, (zero_sum, zero_sum), (image_feats, text_feats))
    return (outputs[0], outputs[1], jnp.stack(totals, axis=1))
```

```python
import functools

import jax
import jax.numpy as jnp
from jax import lax
from jax.experimental import pallas as pl
from jax.experimental.pallas import tpu as pltpu
from jax.sharding import Mesh
from jax.sharding import PartitionSpec as P

EPSILON = 1e-06
F32 = jnp.float32
BF16 = jnp.bfloat16

BLK = ("z", "ylo")
REP = ("yhi", "x", "core")
NZ, NYLO, NYHI, NX, NCORE = 8, 2, 2, 4, 2
D = 1152
ROWS = 128
LANES = 128
MAIN = 2 * LANES
TAIL_AT = NX * MAIN
SENT = MAIN + LANES
PER_BLK = D // (NZ * NYLO)
TAIL_ROWS = PER_BLK // (NX * NYHI)
PIECE = 88
PIECES = NZ * NYLO * NYHI
MIB = 1024 * 1024


def call(kernel, name, out_shape, args, in_specs=None, scratch=(), mib=24, flops=0, moved=0):
    return pl.pallas_call(
        kernel,
        out_shape=out_shape,
        in_specs=in_specs or [pl.BlockSpec(memory_space=pltpu.VMEM)] * len(args),
        scratch_shapes=list(scratch),
        compiler_params=pltpu.CompilerParams(vmem_limit_bytes=mib * MIB),
        cost_estimate=pl.CostEstimate(flops=flops, bytes_accessed=moved, transcendentals=0),
        name=name,
    )(*args)


def shape(dims, dtype=BF16):
    return jax.ShapeDtypeStruct(dims, dtype)


VMEM_SPEC = pl.BlockSpec(memory_space=pltpu.VMEM)
SMEM_SPEC = pl.BlockSpec(memory_space=pltpu.SMEM)


def nt(left, right):
    return lax.dot_general(left, right, (((1,), (1,)), ((), ())), preferred_element_type=F32)


def nn(left, right):
    return lax.dot_general(left, right, (((1,), (0,)), ((), ())), preferred_element_type=F32)


def pick(flag, if_zero, if_one):
    return jnp.where(flag == 0, if_zero, if_one)


def project_kernel(image, text, image_head, text_head, emb_u, emb_v, unit_u, unit_v, norm_u, norm_v):
    col = lax.axis_index("ylo")

    def project(rows, head):
        pre = nn(rows[...], head[...])
        norm = jnp.sqrt(jnp.sum(pre * pre, axis=1, keepdims=True) + EPSILON)
        return pre / norm, norm

    image_unit, image_norm = project(image, image_head)
    text_unit, text_norm = project(text, text_head)
    u = pick(col, text_unit, image_unit)
    v = pick(col, image_unit, text_unit)
    emb_u[...] = u.astype(BF16)
    emb_v[...] = v.astype(BF16)
    unit_u[...] = u
    unit_v[...] = v
    norm_u[...] = pick(col, text_norm, image_norm)
    norm_v[...] = pick(col, image_norm, text_norm)


def turn_kernel(image, text, turned):
    core = lax.axis_index("core")
    image_t = image[...].astype(F32).T
    text_t = text[...].astype(F32).T
    turned[0] = pick(core, image_t, text_t).astype(BF16)
    turned[1] = pick(core, text_t, image_t).astype(BF16)


def pair_weights(own, other, scalars, same):
    scale = jnp.exp(scalars[0])
    logits = scale * nt(own, other) + scalars[1]
    probs = jax.nn.sigmoid(logits)
    if same:
        row = lax.broadcasted_iota(jnp.int32, probs.shape, 0)
        column = lax.broadcasted_iota(jnp.int32, probs.shape, 1)
        probs = probs - jnp.where(row == column, 1.0, 0.0)
    return (scale * probs).astype(BF16)


def pull(own, other, scalars, same=False):
    return nn(pair_weights(own, other, scalars, same), other)


def early_kernel(scalars, u, v, u1, v1, v0, u2, grad_u, grad_v):
    own_u, own_v = u[...], v[...]
    grad_u[...] = (
        pull(own_u, own_v, scalars, True)
        + pull(own_u, v0[...], scalars)
        + pull(own_u, v1[...], scalars)
    )
    grad_v[...] = (
        pull(own_v, own_u, scalars, True)
        + pull(own_v, u1[...], scalars)
        + pull(own_v, u2[...], scalars)
    )


def late_kernel(
    scalars, u, v, u3, v3, grad_u, grad_v, unit_u, unit_v, norm_u, norm_v,
    image_dpre, text_dpre, sent0, sent1, sent2, sent3, mine_t, other_t,
):
    col = lax.axis_index("ylo")
    core = lax.axis_index("core")
    at = lax.axis_index("x")

    def backward(grad, unit, norm):
        radial = jnp.sum(unit * grad, axis=1, keepdims=True)
        return (grad - unit * radial) / norm

    dpre_u = backward(grad_u[...] + pull(u[...], v3[...], scalars), unit_u[...], norm_u[...])
    dpre_v = backward(grad_v[...] + pull(v[...], u3[...], scalars), unit_v[...], norm_v[...])
    image = pick(col, dpre_v, dpre_u)
    text = pick(col, dpre_u, dpre_v)
    image_dpre[...] = image.astype(BF16)
    text_dpre[...] = text.astype(BF16)
    mine_t[...] = pick(core, image, text).T.astype(BF16)
    other_t[...] = pick(core, text, image).T.astype(BF16)
    for step, sent in enumerate((sent0, sent1, sent2, sent3)):
        to = lax.rem(at + step, NX)
        rows = pl.ds(pl.multiple_of(to * MAIN, MAIN), MAIN)
        for place, turned in enumerate((mine_t, other_t)):
            sent[place, :MAIN, :] = turned[rows, :]
            sent[place, MAIN:, :] = turned[TAIL_AT:, :]


def feats_grad_kernel(image_dpre, text_dpre, image_head, text_head, image_out, text_out):
    image_out[...] = nt(image_dpre[...], image_head[...]).astype(BF16)
    text_out[...] = nt(text_dpre[...], text_head[...]).astype(BF16)


def side_by_side_kernel(*refs):
    parts, out = refs[:-1], refs[-1]
    for place, part in enumerate(parts):
        out[:, place * ROWS:(place + 1) * ROWS] = part[place % 2]


def head_kernel(feats_t, *refs):
    parts, pieces, right, total, tail = refs[:8], refs[8], refs[9], refs[10], refs[11]
    at = lax.axis_index("x")
    for place, part in enumerate(parts):
        right[:, place * ROWS:(place + 1) * ROWS] = part[place % 2]
    total[...] = nt(feats_t[...], right[...])
    tail[...] = total[:, MAIN:]
    pad = jnp.zeros((PIECE - PER_BLK - TAIL_ROWS, LANES), F32)
    for blk in range(NZ * NYLO):
        rows = slice(blk * PER_BLK, (blk + 1) * PER_BLK)
        for half in range(NYHI):
            start = blk * PER_BLK + (NYHI * at + half) * TAIL_ROWS
            piece = jnp.concatenate(
                [
                    total[rows, half * LANES:(half + 1) * LANES],
                    tail[pl.ds(start, TAIL_ROWS), :],
                    pad,
                ],
                axis=0,
            )
            pieces[blk * NYHI + half] = piece.astype(BF16)


def add_kernel(pieces, out):
    total = pieces[0].astype(F32)
    for place in range(1, PIECES):
        total = total + pieces[place].astype(F32)
    out[...] = total.astype(BF16)


def place_kernel(*refs):
    parts, out = refs[:-1], refs[-1]
    core = lax.axis_index("core")
    at = lax.axis_index("x")
    half_at = lax.axis_index("yhi")
    for place, part in enumerate(parts):
        flip, step = divmod(place, NX)
        came_x = lax.rem(at + NX - step, NX)
        came_half = lax.rem(half_at + flip, NYHI)
        index = NYHI * came_x + came_half
        mine = part[0].astype(F32)
        other = part[1].astype(F32)
        both = jnp.stack([pick(core, mine, other), pick(core, other, mine)], axis=1)
        out[:, :, pl.ds(pl.multiple_of(index * LANES, LANES), LANES)] = both[:PER_BLK]
        out[pl.ds(index * TAIL_ROWS, TAIL_ROWS), :, TAIL_AT:] = both[PER_BLK:PER_BLK + TAIL_ROWS]


def z_shift(array, sign):
    pairs = []
    for z in range(NZ):
        for y in range(NYLO):
            step = sign if y == 0 else -sign
            pairs.append((z * NYLO + y, ((z + step) % NZ) * NYLO + y))
    return lax.ppermute(array, BLK, pairs)


def y_swap(array):
    return lax.ppermute(array, "ylo", [(0, 1), (1, 0)])


def core_swap(array):
    return lax.ppermute(array, "core", [(0, 1), (1, 0)])


def x_turn(array, by):
    return lax.ppermute(array, "x", [(i, (i + by) % NX) for i in range(NX)])


def rep_turn(array, flip, by):
    pairs = []
    for half in range(NYHI):
        for at in range(NX):
            pairs.append((half * NX + at, ((half + flip) % NYHI) * NX + (at + by) % NX))
    return lax.ppermute(array, ("yhi", "x"), pairs)


def body(image_feats, text_feats, image_head, text_head, log_scale, bias):
    image = image_feats[0]
    text = text_feats[0]
    scalars = jnp.concatenate([log_scale, bias])
    block = shape((ROWS, D))
    block32 = shape((ROWS, D), F32)
    column = shape((ROWS, 1), F32)

    u, v, unit_u, unit_v, norm_u, norm_v = call(
        project_kernel, "project", [block, block, block32, block32, column, column],
        (image, text, image_head, text_head), flops=4 * ROWS * D * D, moved=7 * MIB,
    )
    v1 = z_shift(v, -1)
    u1 = z_shift(u, 1)
    v0 = y_swap(u)
    turned = call(turn_kernel, "turn", shape((2, D, ROWS)), (image, text), moved=MIB)
    feats = [turned] + [x_turn(turned, by) for by in (1, 3, 2)]
    feats_across = [core_swap(part) for part in feats]
    u2 = y_swap(v1)
    u3 = z_shift(u2, 1)
    v3 = y_swap(u1)

    grad_u, grad_v = call(
        early_kernel, "early", [block32, block32], (scalars, u, v, u1, v1, v0, u2),
        in_specs=[SMEM_SPEC] + [VMEM_SPEC] * 6, flops=24 * ROWS * ROWS * D, moved=3 * MIB,
    )
    both = [part for pair in zip(feats, feats_across) for part in pair]
    feats_t = call(
        side_by_side_kernel, "side_by_side", shape((D, 8 * ROWS)), both,
        moved=5 * MIB,
    )
    sent = shape((2, SENT, ROWS))
    image_dpre, text_dpre, *parts = call(
        late_kernel, "late", [block, block, sent, sent, sent, sent],
        (scalars, u, v, u3, v3, grad_u, grad_v, unit_u, unit_v, norm_u, norm_v),
        in_specs=[SMEM_SPEC] + [VMEM_SPEC] * 10,
        scratch=[pltpu.VMEM((D, ROWS), BF16)] * 2, flops=8 * ROWS * ROWS * D, moved=4 * MIB,
    )
    parts = [parts[0], x_turn(parts[1], 1), x_turn(parts[3], 3), x_turn(parts[2], 2)]
    parts_across = [core_swap(part) for part in parts]
    image_out, text_out = call(
        feats_grad_kernel, "feats_grad", [block, block],
        (image_dpre, text_dpre, image_head, text_head), flops=4 * ROWS * D * D, moved=7 * MIB,
    )
    both = [part for pair in zip(parts, parts_across) for part in pair]
    pieces = call(
        head_kernel, "head", shape((PIECES, PIECE, LANES)), [feats_t] + both,
        scratch=[
            pltpu.VMEM((SENT, 8 * ROWS), BF16),
            pltpu.VMEM((D, SENT), F32),
            pltpu.VMEM((D, LANES), F32),
        ],
        flops=16 * ROWS * D * SENT, moved=6 * MIB,
    )
    pieces = lax.all_to_all(pieces, ("z", "ylo", "yhi"), 0, 0, tiled=True)
    mine = call(add_kernel, "add", shape((PIECE, LANES)), (pieces,), moved=MIB)
    two = jnp.stack([mine, core_swap(mine)])
    places = [rep_turn(two, flip, by) if flip or by else two for flip in range(NYHI) for by in range(NX)]
    head_grads = call(place_kernel, "place", shape((PER_BLK, 2, D), F32), places, moved=MIB)
    return (image_out[None], text_out[None], head_grads)


def solution(mesh):
    split = Mesh(mesh.devices.reshape(NZ, NYLO, NYHI, NX, NCORE), BLK + REP)
    rows = P(REP, BLK, None)
    return jax.shard_map(
        body,
        mesh=split,
        in_specs=(rows, rows, P(), P(), P(), P()),
        out_specs=(rows, rows, P(BLK, None, None)),
        check_vma=False,
    )
```

```python
import functools

import jax
import jax.numpy as jnp
from jax import lax
from jax.experimental import pallas as pl
from jax.experimental.pallas import tpu as pltpu
from jax.sharding import Mesh
from jax.sharding import PartitionSpec as P

EPSILON = 1e-06
F32 = jnp.float32
BF16 = jnp.bfloat16

BLK = ("z", "ylo")
REP = ("yhi", "x", "core")
NZ, NYLO, NYHI, NX, NCORE = 8, 2, 2, 4, 2
D = 1152
ROWS = 128
LANES = 128
MAIN = 2 * LANES
TAIL_AT = NX * MAIN
SENT = MAIN + LANES
PER_BLK = D // (NZ * NYLO)
TAIL_ROWS = PER_BLK // (NX * NYHI)
PIECE = PER_BLK + TAIL_ROWS
NY = NYLO * NYHI
MIB = 1024 * 1024


def call(kernel, name, out_shape, args, in_specs=None, scratch=(), mib=24):
    return pl.pallas_call(
        kernel,
        out_shape=out_shape,
        in_specs=in_specs or [pl.BlockSpec(memory_space=pltpu.VMEM)] * len(args),
        scratch_shapes=list(scratch),
        compiler_params=pltpu.CompilerParams(vmem_limit_bytes=mib * MIB),
        cost_estimate=pl.CostEstimate(flops=1, bytes_accessed=1, transcendentals=0),
        name=name,
    )(*args)


def shape(dims, dtype=BF16):
    return jax.ShapeDtypeStruct(dims, dtype)


VMEM_SPEC = pl.BlockSpec(memory_space=pltpu.VMEM)
HBM_SPEC = pl.BlockSpec(memory_space=pltpu.HBM)
SMEM_SPEC = pl.BlockSpec(memory_space=pltpu.SMEM)


def nt(left, right):
    return lax.dot_general(left, right, (((1,), (1,)), ((), ())), preferred_element_type=F32)


def nn(left, right):
    return lax.dot_general(left, right, (((1,), (0,)), ((), ())), preferred_element_type=F32)


def pick(flag, if_zero, if_one):
    return jnp.where(flag == 0, if_zero, if_one)


def project(rows, head):
    pre = nn(rows, head[...])
    norm = jnp.sqrt(jnp.sum(pre * pre, axis=1, keepdims=True) + EPSILON)
    return pre / norm, norm


def choose_kernel(image, text, both, raw_u):
    core = lax.axis_index("core")
    both[0] = pick(core, image[...], text[...])
    both[1] = pick(core, text[...], image[...])
    raw_u[...] = pick(lax.axis_index("ylo"), text[...], image[...])


def pack_feats_kernel(both, across, packed):
    packed[0] = both[0]
    packed[1] = across[1]


def project_kernel(
    image, text, image_head_hbm, text_head_hbm,
    emb_u, emb_v, unit_u, unit_v, norm_u, norm_v, image_head, text_head, sems,
):
    col = lax.axis_index("ylo")
    image_copy = pltpu.make_async_copy(image_head_hbm, image_head, sems.at[0])
    text_copy = pltpu.make_async_copy(text_head_hbm, text_head, sems.at[1])
    image_copy.start()
    text_copy.start()
    image_copy.wait()
    image_unit, image_norm = project(image[...], image_head)
    text_copy.wait()
    text_unit, text_norm = project(text[...], text_head)
    u = pick(col, text_unit, image_unit)
    v = pick(col, image_unit, text_unit)
    emb_u[...] = u.astype(BF16)
    emb_v[...] = v.astype(BF16)
    unit_u[...] = u
    unit_v[...] = v
    norm_u[...] = pick(col, text_norm, image_norm)
    norm_v[...] = pick(col, image_norm, text_norm)


def project_came_kernel(image, text, image_head, text_head, emb_u, emb_v):
    col = lax.axis_index("ylo")
    images = project(image[...], image_head)[0].astype(BF16)
    texts = project(text[...], text_head)[0].astype(BF16)
    emb_u[...] = pick(col, texts, images)
    emb_v[...] = pick(col, images, texts)


def turn_kernel(*refs):
    parts, turned = refs[:-1], refs[-1]
    blocks = [part[side] for part in parts[:-2] for side in range(NCORE)]
    blocks += [part[...] for part in parts[-2:]]
    for place, rows in enumerate(blocks):
        turned[:, place * ROWS:(place + 1) * ROWS] = rows.astype(F32).T.astype(BF16)


def pair_weights(own, other, scalars, same):
    scale = jnp.exp(scalars[0])
    logits = scale * nt(own, other) + scalars[1]
    probs = jax.nn.sigmoid(logits)
    if same:
        row = lax.broadcasted_iota(jnp.int32, probs.shape, 0)
        column = lax.broadcasted_iota(jnp.int32, probs.shape, 1)
        probs = probs - jnp.where(row == column, 1.0, 0.0)
    return (scale * probs).astype(BF16)


def pull(own, other, scalars, same=False):
    return nn(pair_weights(own, other, scalars, same), other)


def early_kernel(scalars, u, v, u1, v1, raw_v0, image_head, text_head, grad_u, grad_v, emb_v0):
    col = lax.axis_index("ylo")

    @pl.when(col == 0)
    def _():
        emb_v0[...] = project(raw_v0[...], image_head)[0].astype(BF16)

    @pl.when(col == 1)
    def _():
        emb_v0[...] = project(raw_v0[...], text_head)[0].astype(BF16)

    own_u, own_v = u[...], v[...]
    grad_u[...] = (
        pull(own_u, own_v, scalars, True)
        + pull(own_u, v1[...], scalars)
        + pull(own_u, emb_v0[...], scalars)
    )
    grad_v[...] = pull(own_v, own_u, scalars, True) + pull(own_v, u1[...], scalars)


def middle_kernel(scalars, v, u2, grad_v, out):
    out[...] = grad_v[...] + pull(v[...], u2[...], scalars)


def late_kernel(
    scalars, u, v, u3, v3, grad_u, grad_v, unit_u, unit_v, norm_u, norm_v,
    image_dpre, text_dpre, mine_parts, other_parts, mine_t, other_t,
):
    col = lax.axis_index("ylo")
    core = lax.axis_index("core")
    at = lax.axis_index("x")

    def backward(grad, unit, norm):
        radial = jnp.sum(unit * grad, axis=1, keepdims=True)
        return (grad - unit * radial) / norm

    dpre_u = backward(grad_u[...] + pull(u[...], v3[...], scalars), unit_u[...], norm_u[...])
    dpre_v = backward(grad_v[...] + pull(v[...], u3[...], scalars), unit_v[...], norm_v[...])
    image = pick(col, dpre_v, dpre_u)
    text = pick(col, dpre_u, dpre_v)
    image_dpre[...] = image.astype(BF16)
    text_dpre[...] = text.astype(BF16)
    mine_t[...] = pick(core, image, text).T.astype(BF16)
    other_t[...] = pick(core, text, image).T.astype(BF16)
    for step in range(NX):
        to = lax.rem(at + step, NX)
        rows = pl.ds(pl.multiple_of(to * MAIN, MAIN), MAIN)
        for turned, parts in ((mine_t, mine_parts), (other_t, other_parts)):
            parts[step, :MAIN, :] = turned[rows, :]
            parts[step, MAIN:, :] = turned[TAIL_AT:, :]


def pack_parts_kernel(mine, across, *packed):
    for step, part in enumerate(packed):
        part[0] = mine[step]
        part[1] = across[step]


def feats_grad_kernel(image_dpre, text_dpre, image_head, text_head, image_out, text_out):
    image_out[...] = nt(image_dpre[...], image_head[...]).astype(BF16)
    text_out[...] = nt(text_dpre[...], text_head[...]).astype(BF16)


def head_kernel(feats_t, *refs):
    parts, pieces, right, total, tails = refs[:NX], refs[NX:NX + NY], *refs[NX + NY:]
    at = lax.axis_index("x")
    y = NYLO * lax.axis_index("yhi") + lax.axis_index("ylo")
    for place, part in enumerate(parts):
        for side in range(NCORE):
            start = (place * NCORE + side) * ROWS
            right[:, start:start + ROWS] = part[side]
    total[...] = nt(feats_t[...], right[...])
    tails[...] = total[:, MAIN:]
    for step, piece in enumerate(pieces):
        to = lax.rem(y + step, NY)
        half, low = to // NYLO, lax.rem(to, NYLO)
        lanes = pl.ds(pl.multiple_of(half * LANES, LANES), LANES)
        for z in range(NZ):
            start = pl.multiple_of((z * NYLO + low) * PER_BLK, 8)
            tail = start + (NYHI * at + half) * TAIL_ROWS
            rows = [
                total[pl.ds(start, PER_BLK), lanes],
                tails[pl.ds(tail, TAIL_ROWS), :],
            ]
            piece[z] = jnp.concatenate(rows, axis=0).astype(BF16)


def add_kernel(*refs):
    parts, out = refs[:-1], refs[-1]
    total = parts[0][...].astype(F32)
    for part in parts[1:]:
        total = total + part[...].astype(F32)
    out[...] = total.astype(BF16)


def add_z_kernel(pieces, out):
    total = pieces[0].astype(F32)
    for place in range(1, NZ):
        total = total + pieces[place].astype(F32)
    out[...] = total.astype(BF16)


def place_kernel(*refs):
    parts, out = refs[:-1], refs[-1]
    core = lax.axis_index("core")
    at = lax.axis_index("x")
    half_at = lax.axis_index("yhi")
    for step, part in enumerate(parts):
        came_x = lax.rem(at + NX - step, NX)
        for flip in range(NYHI):
            index = NYHI * came_x + lax.rem(half_at + flip, NYHI)
            mine = part[flip, 0].astype(F32)
            other = part[flip, 1].astype(F32)
            both = jnp.stack([pick(core, mine, other), pick(core, other, mine)], axis=1)
            out[:, :, pl.ds(pl.multiple_of(index * LANES, LANES), LANES)] = both[:PER_BLK]
            out[pl.ds(index * TAIL_ROWS, TAIL_ROWS), :, TAIL_AT:] = both[PER_BLK:PER_BLK + TAIL_ROWS]


def z_shift(array, by):
    return lax.ppermute(array, "z", [(z, (z + by) % NZ) for z in range(NZ)])


def u_shift(array):
    pairs = []
    for z in range(NZ):
        pairs.append((z * NYLO, ((z + 1) % NZ) * NYLO))
        pairs.append((z * NYLO + 1, ((z - 1) % NZ) * NYLO + 1))
    return lax.ppermute(array, BLK, pairs)


def y_swap(array):
    return lax.ppermute(array, "ylo", [(0, 1), (1, 0)])


def core_swap(array):
    return lax.ppermute(array, "core", [(0, 1), (1, 0)])


def x_turn(array, by):
    return lax.ppermute(array, "x", [(i, (i + by) % NX) for i in range(NX)])


def y_turn(array, by):
    index = lambda y: (y % NYLO) * NYHI + y // NYLO
    pairs = [(index(y), index((y + by) % NY)) for y in range(NY)]
    return lax.ppermute(array, ("ylo", "yhi"), pairs)


def half_swap(array, flip, swap):
    pairs = []
    for half in range(NYHI):
        for x in range(NX):
            for core in range(NCORE):
                start = (half * NX + x) * NCORE + core
                pairs.append((start, ((half ^ flip) * NX + x) * NCORE + (core ^ swap)))
    return lax.ppermute(array, REP, pairs)


def body(image_feats, text_feats, image_head, text_head, log_scale, bias):
    image = image_feats[0]
    text = text_feats[0]
    scalars = jnp.concatenate([log_scale, bias])
    block = shape((ROWS, D))
    block32 = shape((ROWS, D), F32)
    column = shape((ROWS, 1), F32)

    text_1 = z_shift(text, 1)
    image_1 = z_shift(image, -1)
    both, raw_u = call(choose_kernel, "choose", [shape((2, ROWS, D)), block], (image, text))
    raw_v0 = y_swap(raw_u)
    packed = call(pack_feats_kernel, "pack_feats", shape((2, ROWS, D)), (both, core_swap(both)))
    feats_1, feats_3 = x_turn(packed, 1), x_turn(packed, 3)
    u, v, unit_u, unit_v, norm_u, norm_v, image_head, text_head = call(
        project_kernel, "project",
        [block, block, block32, block32, column, column, shape((D, D)), shape((D, D))],
        (image, text, image_head, text_head),
        in_specs=[VMEM_SPEC] * 2 + [HBM_SPEC] * 2,
        scratch=[pltpu.SemaphoreType.DMA((2,))], mib=46,
    )
    image_1, text_1, raw_v0, packed = lax.optimization_barrier((image_1, text_1, raw_v0, packed))
    u1, v1 = call(
        project_came_kernel, "project_came", [block, block],
        (image_1, text_1, image_head, text_head),
    )
    u2 = y_swap(v1)
    v3 = y_swap(u1)
    raw_v0, u1 = lax.optimization_barrier((raw_v0, u1))
    grad_u, grad_v = call(
        early_kernel, "early", [block32, block32],
        (scalars, u, v, u1, v1, raw_v0, image_head, text_head),
        in_specs=[SMEM_SPEC] + [VMEM_SPEC] * 7,
        scratch=[pltpu.VMEM((ROWS, D), BF16)],
    )
    u2, grad_u, grad_v, feats_1, feats_3 = lax.optimization_barrier(
        (u2, grad_u, grad_v, feats_1, feats_3)
    )
    u3 = u_shift(u2)
    feats_2 = (x_turn(feats_1[0], 1), x_turn(feats_3[1], 3))
    grad_v = call(
        middle_kernel, "middle", block32, (scalars, v, u2, grad_v),
        in_specs=[SMEM_SPEC] + [VMEM_SPEC] * 3,
    )
    u3, v3, feats_2 = lax.optimization_barrier((u3, v3, feats_2))
    parts = shape((NX, SENT, ROWS))
    image_dpre, text_dpre, mine_parts, other_parts = call(
        late_kernel, "late", [block, block, parts, parts],
        (scalars, u, v, u3, v3, grad_u, grad_v, unit_u, unit_v, norm_u, norm_v),
        in_specs=[SMEM_SPEC] + [VMEM_SPEC] * 10,
        scratch=[pltpu.VMEM((D, ROWS), BF16)] * 2,
    )
    across = core_swap(other_parts)
    parts = call(
        pack_parts_kernel, "pack_parts", [shape((2, SENT, ROWS))] * NX, (mine_parts, across)
    )
    feats_1, feats_2, feats_3, image_dpre, text_dpre = lax.optimization_barrier(
        (feats_1, feats_2, feats_3, image_dpre, text_dpre)
    )
    image_out, text_out = call(
        feats_grad_kernel, "feats_grad", [block, block],
        (image_dpre, text_dpre, image_head, text_head),
    )
    feats_t = call(
        turn_kernel, "turn", shape((D, NX * NCORE * ROWS)), (packed, feats_1, feats_3, *feats_2)
    )
    came = [x_turn(parts[1], 1), x_turn(parts[3], 3), x_turn(parts[2], 2)]
    came, image_out, text_out, feats_t = lax.optimization_barrier(
        (came, image_out, text_out, feats_t)
    )
    pieces = call(
        head_kernel, "head", [shape((NZ, PIECE, LANES))] * NY, [feats_t, parts[0]] + came,
        scratch=[
            pltpu.VMEM((SENT, NX * NCORE * ROWS), BF16),
            pltpu.VMEM((D, SENT), F32),
            pltpu.VMEM((D, LANES), F32),
        ],
    )
    pieces = [pieces[0]] + [y_turn(pieces[by], by) for by in (2, 1, 3)]
    pieces = call(add_kernel, "add_y", shape((NZ, PIECE, LANES)), pieces)
    pieces = lax.all_to_all(pieces, "z", 0, 0, tiled=True)
    mine = call(add_z_kernel, "add_z", shape((PIECE, LANES)), (pieces,))
    four = jnp.stack([mine] + [half_swap(mine, flip, swap) for flip, swap in ((0, 1), (1, 0), (1, 1))])
    four = four.reshape(NYHI, NCORE, PIECE, LANES)
    places = [four] + [x_turn(four, by) for by in (1, 2, 3)]
    head_grads = call(place_kernel, "place", shape((PER_BLK, 2, D), F32), places)
    return (image_out[None], text_out[None], head_grads)


def solution(mesh):
    split = Mesh(mesh.devices.reshape(NZ, NYLO, NYHI, NX, NCORE), BLK + REP)
    rows = P(REP, BLK, None)
    return jax.shard_map(
        body,
        mesh=split,
        in_specs=(rows, rows, P(), P(), P(), P()),
        out_specs=(rows, rows, P(BLK, None, None)),
        check_vma=False,
    )
```

```python
import functools

import jax
import jax.numpy as jnp
from jax import lax
from jax.experimental import pallas as pl
from jax.experimental.pallas import tpu as pltpu
from jax.sharding import Mesh
from jax.sharding import PartitionSpec as P

EPSILON = 1e-06
F32 = jnp.float32
BF16 = jnp.bfloat16

BLK = ("z", "ylo")
REP = ("yhi", "x", "core")
NZ, NYLO, NYHI, NX, NCORE = 8, 2, 2, 4, 2
D = 1152
ROWS = 128
LANES = 128
MAIN = 2 * LANES
TAIL_AT = NX * MAIN
SENT = MAIN + LANES
PER_BLK = D // (NZ * NYLO)
TAIL_ROWS = PER_BLK // (NX * NYHI)
PIECE = PER_BLK + TAIL_ROWS
NY = NYLO * NYHI
MIB = 1024 * 1024


def call(kernel, name, out_shape, args, in_specs=None, scratch=(), mib=24):
    return pl.pallas_call(
        kernel,
        out_shape=out_shape,
        in_specs=in_specs or [pl.BlockSpec(memory_space=pltpu.VMEM)] * len(args),
        scratch_shapes=list(scratch),
        compiler_params=pltpu.CompilerParams(vmem_limit_bytes=mib * MIB),
        cost_estimate=pl.CostEstimate(flops=1, bytes_accessed=1, transcendentals=0),
        name=name,
    )(*args)


def shape(dims, dtype=BF16):
    return jax.ShapeDtypeStruct(dims, dtype)


VMEM_SPEC = pl.BlockSpec(memory_space=pltpu.VMEM)
HBM_SPEC = pl.BlockSpec(memory_space=pltpu.HBM)
SMEM_SPEC = pl.BlockSpec(memory_space=pltpu.SMEM)


def nt(left, right):
    return lax.dot_general(left, right, (((1,), (1,)), ((), ())), preferred_element_type=F32)


def nn(left, right):
    return lax.dot_general(left, right, (((1,), (0,)), ((), ())), preferred_element_type=F32)


def pick(flag, if_zero, if_one):
    return jnp.where(flag == 0, if_zero, if_one)


def project(rows, head):
    pre = nn(rows, head[...])
    norm = jnp.sqrt(jnp.sum(pre * pre, axis=1, keepdims=True) + EPSILON)
    return pre / norm, norm


def choose_kernel(image, text, both, raw_u):
    core = lax.axis_index("core")
    both[0] = pick(core, image[...], text[...])
    both[1] = pick(core, text[...], image[...])
    raw_u[...] = pick(lax.axis_index("ylo"), text[...], image[...])


def pack_feats_kernel(both, across, packed):
    packed[0] = both[0]
    packed[1] = across[1]


def load_kernel(image_head_hbm, text_head_hbm, image_head, text_head, sems):
    copies = [
        pltpu.make_async_copy(image_head_hbm, image_head, sems.at[0]),
        pltpu.make_async_copy(text_head_hbm, text_head, sems.at[1]),
    ]
    for copy in copies:
        copy.start()
    for copy in copies:
        copy.wait()


def project_kernel(both, image_head, text_head, emb_u, emb_v, unit_u, unit_v, norm_u, norm_v):
    col = lax.axis_index("ylo")
    core = lax.axis_index("core")
    image_unit, image_norm = project(pick(core, both[0], both[1]), image_head)
    text_unit, text_norm = project(pick(core, both[1], both[0]), text_head)
    u = pick(col, text_unit, image_unit)
    v = pick(col, image_unit, text_unit)
    emb_u[...] = u.astype(BF16)
    emb_v[...] = v.astype(BF16)
    unit_u[...] = u
    unit_v[...] = v
    norm_u[...] = pick(col, text_norm, image_norm)
    norm_v[...] = pick(col, image_norm, text_norm)


def project_came_kernel(image, text, image_head, text_head, emb_u, emb_v):
    col = lax.axis_index("ylo")
    images = project(image[...], image_head)[0].astype(BF16)
    texts = project(text[...], text_head)[0].astype(BF16)
    emb_u[...] = pick(col, texts, images)
    emb_v[...] = pick(col, images, texts)


def turn_kernel(*refs):
    parts, turned = refs[:-1], refs[-1]
    blocks = [part[side] for part in parts[:-2] for side in range(NCORE)]
    blocks += [part[...] for part in parts[-2:]]
    for place, rows in enumerate(blocks):
        turned[:, place * ROWS:(place + 1) * ROWS] = rows.astype(F32).T.astype(BF16)


def pair_weights(own, other, scalars, same):
    scale = jnp.exp(scalars[0])
    logits = scale * nt(own, other) + scalars[1]
    probs = jax.nn.sigmoid(logits)
    if same:
        row = lax.broadcasted_iota(jnp.int32, probs.shape, 0)
        column = lax.broadcasted_iota(jnp.int32, probs.shape, 1)
        probs = probs - jnp.where(row == column, 1.0, 0.0)
    return (scale * probs).astype(BF16)


def pull(own, other, scalars, same=False):
    return nn(pair_weights(own, other, scalars, same), other)


def early_kernel(scalars, u, v, u1, v1, raw_v0, image_head, text_head, grad_u, grad_v, emb_v0):
    col = lax.axis_index("ylo")

    @pl.when(col == 0)
    def _():
        emb_v0[...] = project(raw_v0[...], image_head)[0].astype(BF16)

    @pl.when(col == 1)
    def _():
        emb_v0[...] = project(raw_v0[...], text_head)[0].astype(BF16)

    own_u, own_v = u[...], v[...]
    grad_u[...] = (
        pull(own_u, own_v, scalars, True)
        + pull(own_u, v1[...], scalars)
        + pull(own_u, emb_v0[...], scalars)
    )
    grad_v[...] = pull(own_v, own_u, scalars, True) + pull(own_v, u1[...], scalars)


def middle_kernel(scalars, v, u2, grad_v, out):
    out[...] = grad_v[...] + pull(v[...], u2[...], scalars)


def late_kernel(
    scalars, u, v, u3, v3, grad_u, grad_v, unit_u, unit_v, norm_u, norm_v,
    image_dpre, text_dpre, sent0, sent1, sent2, sent3, mine_t, other_t,
):
    col = lax.axis_index("ylo")
    core = lax.axis_index("core")
    at = lax.axis_index("x")

    def backward(grad, unit, norm):
        radial = jnp.sum(unit * grad, axis=1, keepdims=True)
        return (grad - unit * radial) / norm

    dpre_u = backward(grad_u[...] + pull(u[...], v3[...], scalars), unit_u[...], norm_u[...])
    dpre_v = backward(grad_v[...] + pull(v[...], u3[...], scalars), unit_v[...], norm_v[...])
    image = pick(col, dpre_v, dpre_u)
    text = pick(col, dpre_u, dpre_v)
    image_dpre[...] = image.astype(BF16)
    text_dpre[...] = text.astype(BF16)
    mine_t[...] = pick(core, image, text).T.astype(BF16)
    other_t[...] = pick(core, text, image).T.astype(BF16)
    for step, sent in enumerate((sent0, sent1, sent2, sent3)):
        to = lax.rem(at + step, NX)
        rows = pl.ds(pl.multiple_of(to * MAIN, MAIN), MAIN)
        for place, turned in enumerate((mine_t, other_t)):
            sent[place, :MAIN, :] = turned[rows, :]
            sent[place, MAIN:, :] = turned[TAIL_AT:, :]


def others_kernel(*refs):
    parts, others = refs[:-1], refs[-1]
    for step, part in enumerate(parts):
        others[step] = part[1]


def feats_grad_kernel(image_dpre, text_dpre, image_head, text_head, image_out, text_out):
    image_out[...] = nt(image_dpre[...], image_head[...]).astype(BF16)
    text_out[...] = nt(text_dpre[...], text_head[...]).astype(BF16)


def head_kernel(feats_t, *refs):
    across, parts, refs = refs[0], refs[1:NX + 1], refs[NX + 1:]
    pieces, right, total, tails = refs[:NY], *refs[NY:]
    at = lax.axis_index("x")
    y = NYLO * lax.axis_index("yhi") + lax.axis_index("ylo")
    for place, part in enumerate(parts):
        start = place * NCORE * ROWS
        right[:, start:start + ROWS] = part[0]
        right[:, start + ROWS:start + 2 * ROWS] = across[place]
    total[...] = nt(feats_t[...], right[...])
    tails[...] = total[:, MAIN:]
    for step, piece in enumerate(pieces):
        to = lax.rem(y + step, NY)
        half, low = to // NYLO, lax.rem(to, NYLO)
        lanes = pl.ds(pl.multiple_of(half * LANES, LANES), LANES)
        for z in range(NZ):
            start = pl.multiple_of((z * NYLO + low) * PER_BLK, 8)
            tail = start + (NYHI * at + half) * TAIL_ROWS
            rows = [
                total[pl.ds(start, PER_BLK), lanes],
                tails[pl.ds(tail, TAIL_ROWS), :],
            ]
            piece[z] = jnp.concatenate(rows, axis=0).astype(BF16)


def add_kernel(*refs):
    parts, out = refs[:-1], refs[-1]
    total = parts[0][...].astype(F32)
    for part in parts[1:]:
        total = total + part[...].astype(F32)
    out[...] = total.astype(BF16)


def add_z_kernel(pieces, out):
    total = pieces[0].astype(F32)
    for place in range(1, NZ):
        total = total + pieces[place].astype(F32)
    out[...] = total.astype(BF16)


def place_kernel(*refs):
    parts, out = refs[:-1], refs[-1]
    core = lax.axis_index("core")
    at = lax.axis_index("x")
    half_at = lax.axis_index("yhi")
    for step, part in enumerate(parts):
        came_x = lax.rem(at + NX - step, NX)
        for flip in range(NYHI):
            index = NYHI * came_x + lax.rem(half_at + flip, NYHI)
            mine = part[flip, 0].astype(F32)
            other = part[flip, 1].astype(F32)
            both = jnp.stack([pick(core, mine, other), pick(core, other, mine)], axis=1)
            out[:, :, pl.ds(pl.multiple_of(index * LANES, LANES), LANES)] = both[:PER_BLK]
            out[pl.ds(index * TAIL_ROWS, TAIL_ROWS), :, TAIL_AT:] = both[PER_BLK:PER_BLK + TAIL_ROWS]


def z_shift(array, by):
    return lax.ppermute(array, "z", [(z, (z + by) % NZ) for z in range(NZ)])


def u_shift(array):
    pairs = []
    for z in range(NZ):
        pairs.append((z * NYLO, ((z + 1) % NZ) * NYLO))
        pairs.append((z * NYLO + 1, ((z - 1) % NZ) * NYLO + 1))
    return lax.ppermute(array, BLK, pairs)


def y_swap(array):
    return lax.ppermute(array, "ylo", [(0, 1), (1, 0)])


def core_swap(array):
    return lax.ppermute(array, "core", [(0, 1), (1, 0)])


def x_turn(array, by):
    return lax.ppermute(array, "x", [(i, (i + by) % NX) for i in range(NX)])


def y_turn(array, by):
    index = lambda y: (y % NYLO) * NYHI + y // NYLO
    pairs = [(index(y), index((y + by) % NY)) for y in range(NY)]
    return lax.ppermute(array, ("ylo", "yhi"), pairs)


def half_swap(array, flip, swap):
    pairs = []
    for half in range(NYHI):
        for x in range(NX):
            for core in range(NCORE):
                start = (half * NX + x) * NCORE + core
                pairs.append((start, ((half ^ flip) * NX + x) * NCORE + (core ^ swap)))
    return lax.ppermute(array, REP, pairs)


def body(image_feats, text_feats, image_head, text_head, log_scale, bias):
    image = image_feats[0]
    text = text_feats[0]
    scalars = jnp.concatenate([log_scale, bias])
    block = shape((ROWS, D))
    block32 = shape((ROWS, D), F32)
    column = shape((ROWS, 1), F32)

    text_1 = z_shift(text, 1)
    image_1 = z_shift(image, -1)
    both, raw_u = call(choose_kernel, "choose", [shape((2, ROWS, D)), block], (image, text))
    raw_v0 = y_swap(raw_u)
    packed = call(pack_feats_kernel, "pack_feats", shape((2, ROWS, D)), (both, core_swap(both)))
    feats_1, feats_3 = x_turn(packed, 1), x_turn(packed, 3)
    image_head, text_head = call(
        load_kernel, "load", [shape((D, D)), shape((D, D))], (image_head, text_head),
        in_specs=[HBM_SPEC] * 2, scratch=[pltpu.SemaphoreType.DMA((2,))], mib=46,
    )
    image_1, text_1, packed = lax.optimization_barrier((image_1, text_1, packed))
    u1, v1 = call(
        project_came_kernel, "project_came", [block, block],
        (image_1, text_1, image_head, text_head),
    )
    u2 = y_swap(v1)
    raw_v0, both, u1 = lax.optimization_barrier((raw_v0, both, u1))
    u, v, unit_u, unit_v, norm_u, norm_v = call(
        project_kernel, "project", [block, block, block32, block32, column, column],
        (both, image_head, text_head),
    )
    grad_u, grad_v = call(
        early_kernel, "early", [block32, block32],
        (scalars, u, v, u1, v1, raw_v0, image_head, text_head),
        in_specs=[SMEM_SPEC] + [VMEM_SPEC] * 7,
        scratch=[pltpu.VMEM((ROWS, D), BF16)],
    )
    u2, u1, grad_u, grad_v, feats_1, feats_3 = lax.optimization_barrier(
        (u2, u1, grad_u, grad_v, feats_1, feats_3)
    )
    u3 = u_shift(u2)
    v3 = y_swap(u1)
    feats_2 = (x_turn(feats_1[0], 1), x_turn(feats_3[1], 3))
    grad_v = call(
        middle_kernel, "middle", block32, (scalars, v, u2, grad_v),
        in_specs=[SMEM_SPEC] + [VMEM_SPEC] * 3,
    )
    sent = shape((2, SENT, ROWS))
    image_dpre, text_dpre, *parts = call(
        late_kernel, "late", [block, block, sent, sent, sent, sent],
        (scalars, u, v, u3, v3, grad_u, grad_v, unit_u, unit_v, norm_u, norm_v),
        in_specs=[SMEM_SPEC] + [VMEM_SPEC] * 10,
        scratch=[pltpu.VMEM((D, ROWS), BF16)] * 2,
    )
    parts, feats_2 = lax.optimization_barrier((parts, feats_2))
    image_out, text_out = call(
        feats_grad_kernel, "feats_grad", [block, block],
        (image_dpre, text_dpre, image_head, text_head),
    )
    feats_t = call(
        turn_kernel, "turn", shape((D, NX * NCORE * ROWS)), (packed, feats_1, feats_3, *feats_2)
    )
    came = [x_turn(parts[1], 1), x_turn(parts[3], 3), x_turn(parts[2], 2)]
    came, image_out, text_out, feats_t = lax.optimization_barrier(
        (came, image_out, text_out, feats_t)
    )
    parts = [parts[0]] + came
    others = call(others_kernel, "others", shape((NX, SENT, ROWS)), parts)
    pieces = call(
        head_kernel, "head", [shape((NZ, PIECE, LANES))] * NY,
        [feats_t, core_swap(others)] + parts,
        scratch=[
            pltpu.VMEM((SENT, NX * NCORE * ROWS), BF16),
            pltpu.VMEM((D, SENT), F32),
            pltpu.VMEM((D, LANES), F32),
        ],
    )
    pieces = [pieces[0]] + [y_turn(pieces[by], by) for by in (2, 1, 3)]
    pieces = call(add_kernel, "add_y", shape((NZ, PIECE, LANES)), pieces)
    pieces = lax.all_to_all(pieces, "z", 0, 0, tiled=True)
    mine = call(add_z_kernel, "add_z", shape((PIECE, LANES)), (pieces,))
    four = jnp.stack([mine] + [half_swap(mine, flip, swap) for flip, swap in ((0, 1), (1, 0), (1, 1))])
    four = four.reshape(NYHI, NCORE, PIECE, LANES)
    places = [four] + [x_turn(four, by) for by in (1, 2, 3)]
    head_grads = call(place_kernel, "place", shape((PER_BLK, 2, D), F32), places)
    return (image_out[None], text_out[None], head_grads)


def solution(mesh):
    split = Mesh(mesh.devices.reshape(NZ, NYLO, NYHI, NX, NCORE), BLK + REP)
    rows = P(REP, BLK, None)
    return jax.shard_map(
        body,
        mesh=split,
        in_specs=(rows, rows, P(), P(), P(), P()),
        out_specs=(rows, rows, P(BLK, None, None)),
        check_vma=False,
    )
```

```python
import functools

import jax
import jax.numpy as jnp
from jax import lax
from jax.experimental import pallas as pl
from jax.experimental.pallas import tpu as pltpu
from jax.sharding import Mesh
from jax.sharding import PartitionSpec as P

EPSILON = 1e-06
F32 = jnp.float32
BF16 = jnp.bfloat16

BLK = ("z", "ylo")
REP = ("yhi", "x", "core")
NZ, NYLO, NYHI, NX, NCORE = 8, 2, 2, 4, 2
D = 1152
ROWS = 128
LANES = 128
MAIN = 2 * LANES
TAIL_AT = NX * MAIN
SENT = MAIN + LANES
PER_BLK = D // (NZ * NYLO)
TAIL_ROWS = PER_BLK // (NX * NYHI)
PIECE = PER_BLK + TAIL_ROWS
NY = NYLO * NYHI
MIB = 1024 * 1024


def call(kernel, name, out_shape, args, in_specs=None, scratch=(), mib=24):
    return pl.pallas_call(
        kernel,
        out_shape=out_shape,
        in_specs=in_specs or [pl.BlockSpec(memory_space=pltpu.VMEM)] * len(args),
        scratch_shapes=list(scratch),
        compiler_params=pltpu.CompilerParams(vmem_limit_bytes=mib * MIB),
        cost_estimate=pl.CostEstimate(flops=1, bytes_accessed=1, transcendentals=0),
        name=name,
    )(*args)


def shape(dims, dtype=BF16):
    return jax.ShapeDtypeStruct(dims, dtype)


VMEM_SPEC = pl.BlockSpec(memory_space=pltpu.VMEM)
HBM_SPEC = pl.BlockSpec(memory_space=pltpu.HBM)
SMEM_SPEC = pl.BlockSpec(memory_space=pltpu.SMEM)


def nt(left, right):
    return lax.dot_general(left, right, (((1,), (1,)), ((), ())), preferred_element_type=F32)


def nn(left, right):
    return lax.dot_general(left, right, (((1,), (0,)), ((), ())), preferred_element_type=F32)


def pick(flag, if_zero, if_one):
    return jnp.where(flag == 0, if_zero, if_one)


def project(rows, head):
    pre = nn(rows, head[...])
    norm = jnp.sqrt(jnp.sum(pre * pre, axis=1, keepdims=True) + EPSILON)
    return pre / norm, norm


def choose_kernel(image, text, both, raw_u):
    core = lax.axis_index("core")
    both[0] = pick(core, image[...], text[...])
    both[1] = pick(core, text[...], image[...])
    raw_u[...] = pick(lax.axis_index("ylo"), text[...], image[...])


def pack_feats_kernel(both, across, packed):
    packed[0] = both[0]
    packed[1] = across[1]


def load_kernel(image_head_hbm, text_head_hbm, image_head, text_head, sems):
    copies = [
        pltpu.make_async_copy(image_head_hbm, image_head, sems.at[0]),
        pltpu.make_async_copy(text_head_hbm, text_head, sems.at[1]),
    ]
    for copy in copies:
        copy.start()
    for copy in copies:
        copy.wait()


def project_kernel(both, image_head, text_head, emb_u, emb_v, unit_u, unit_v, norm_u, norm_v):
    col = lax.axis_index("ylo")
    core = lax.axis_index("core")
    image_unit, image_norm = project(pick(core, both[0], both[1]), image_head)
    text_unit, text_norm = project(pick(core, both[1], both[0]), text_head)
    u = pick(col, text_unit, image_unit)
    v = pick(col, image_unit, text_unit)
    emb_u[...] = u.astype(BF16)
    emb_v[...] = v.astype(BF16)
    unit_u[...] = u
    unit_v[...] = v
    norm_u[...] = pick(col, text_norm, image_norm)
    norm_v[...] = pick(col, image_norm, text_norm)


def project_came_kernel(image, text, image_head, text_head, emb_u, emb_v):
    col = lax.axis_index("ylo")
    images = project(image[...], image_head)[0].astype(BF16)
    texts = project(text[...], text_head)[0].astype(BF16)
    emb_u[...] = pick(col, texts, images)
    emb_v[...] = pick(col, images, texts)


def turn_kernel(*refs):
    parts, turned = refs[:-2], refs[-2:]
    blocks = [part[side] for part in parts[:-2] for side in range(NCORE)]
    blocks += [part[...] for part in parts[-2:]]
    for place, rows in enumerate(blocks):
        step, side = divmod(place, NCORE)
        turned[side][:, step * ROWS:(step + 1) * ROWS] = rows.astype(F32).T.astype(BF16)


def pair_weights(own, other, scalars, same):
    scale = jnp.exp(scalars[0])
    logits = scale * nt(own, other) + scalars[1]
    probs = jax.nn.sigmoid(logits)
    if same:
        row = lax.broadcasted_iota(jnp.int32, probs.shape, 0)
        column = lax.broadcasted_iota(jnp.int32, probs.shape, 1)
        probs = probs - jnp.where(row == column, 1.0, 0.0)
    return (scale * probs).astype(BF16)


def pull(own, other, scalars, same=False):
    return nn(pair_weights(own, other, scalars, same), other)


def early_kernel(scalars, u, v, u1, v1, raw_v0, image_head, text_head, grad_u, grad_v, emb_v0):
    col = lax.axis_index("ylo")

    @pl.when(col == 0)
    def _():
        emb_v0[...] = project(raw_v0[...], image_head)[0].astype(BF16)

    @pl.when(col == 1)
    def _():
        emb_v0[...] = project(raw_v0[...], text_head)[0].astype(BF16)

    own_u, own_v = u[...], v[...]
    grad_u[...] = (
        pull(own_u, own_v, scalars, True)
        + pull(own_u, v1[...], scalars)
        + pull(own_u, emb_v0[...], scalars)
    )
    grad_v[...] = pull(own_v, own_u, scalars, True) + pull(own_v, u1[...], scalars)


def middle_kernel(scalars, v, u2, grad_v, out):
    out[...] = grad_v[...] + pull(v[...], u2[...], scalars)


def late_kernel(
    scalars, u, v, u3, v3, grad_u, grad_v, unit_u, unit_v, norm_u, norm_v,
    image_dpre, text_dpre, sent0, sent1, sent2, sent3, mine_t, other_t,
):
    col = lax.axis_index("ylo")
    core = lax.axis_index("core")
    at = lax.axis_index("x")

    def backward(grad, unit, norm):
        radial = jnp.sum(unit * grad, axis=1, keepdims=True)
        return (grad - unit * radial) / norm

    dpre_u = backward(grad_u[...] + pull(u[...], v3[...], scalars), unit_u[...], norm_u[...])
    dpre_v = backward(grad_v[...] + pull(v[...], u3[...], scalars), unit_v[...], norm_v[...])
    image = pick(col, dpre_v, dpre_u)
    text = pick(col, dpre_u, dpre_v)
    image_dpre[...] = image.astype(BF16)
    text_dpre[...] = text.astype(BF16)
    mine_t[...] = pick(core, image, text).T.astype(BF16)
    other_t[...] = pick(core, text, image).T.astype(BF16)
    for step, sent in enumerate((sent0, sent1, sent2, sent3)):
        to = lax.rem(at + step, NX)
        rows = pl.ds(pl.multiple_of(to * MAIN, MAIN), MAIN)
        for place, turned in enumerate((mine_t, other_t)):
            sent[place, :MAIN, :] = turned[rows, :]
            sent[place, MAIN:, :] = turned[TAIL_AT:, :]


def others_kernel(*refs):
    parts, others = refs[:-1], refs[-1]
    for step, part in enumerate(parts):
        others[step] = part[1]


def feats_grad_kernel(image_dpre, text_dpre, image_head, text_head, image_out, text_out):
    image_out[...] = nt(image_dpre[...], image_head[...]).astype(BF16)
    text_out[...] = nt(text_dpre[...], text_head[...]).astype(BF16)


def own_head_kernel(feats_t, *refs):
    parts, total, right = refs[:NX], refs[NX], refs[NX + 1]
    for place, part in enumerate(parts):
        right[:, place * ROWS:(place + 1) * ROWS] = part[0]
    total[...] = nt(feats_t[...], right[...])


def head_kernel(feats_t, across, own, *refs):
    pieces, right, total, tails = refs[:NY], *refs[NY:]
    at = lax.axis_index("x")
    y = NYLO * lax.axis_index("yhi") + lax.axis_index("ylo")
    for place in range(NX):
        right[:, place * ROWS:(place + 1) * ROWS] = across[place]
    total[...] = own[...] + nt(feats_t[...], right[...])
    tails[...] = total[:, MAIN:]
    for step, piece in enumerate(pieces):
        to = lax.rem(y + step, NY)
        half, low = to // NYLO, lax.rem(to, NYLO)
        lanes = pl.ds(pl.multiple_of(half * LANES, LANES), LANES)
        for z in range(NZ):
            start = pl.multiple_of((z * NYLO + low) * PER_BLK, 8)
            tail = start + (NYHI * at + half) * TAIL_ROWS
            rows = [
                total[pl.ds(start, PER_BLK), lanes],
                tails[pl.ds(tail, TAIL_ROWS), :],
            ]
            piece[z] = jnp.concatenate(rows, axis=0).astype(BF16)


def add_kernel(*refs):
    parts, out = refs[:-1], refs[-1]
    total = parts[0][...].astype(F32)
    for part in parts[1:]:
        total = total + part[...].astype(F32)
    out[...] = total.astype(BF16)


def add_z_kernel(pieces, out):
    total = pieces[0].astype(F32)
    for place in range(1, NZ):
        total = total + pieces[place].astype(F32)
    out[...] = total.astype(BF16)


def place_kernel(mine, other, out):
    core = lax.axis_index("core")
    at = lax.axis_index("x")
    half_at = lax.axis_index("yhi")
    for step in range(NX):
        came_x = lax.rem(at + NX - step, NX)
        for flip in range(NYHI):
            index = NYHI * came_x + lax.rem(half_at + flip, NYHI)
            own = mine[step, flip].astype(F32)
            across = other[step, flip].astype(F32)
            lanes = pl.ds(pl.multiple_of(index * LANES, LANES), LANES)
            rows = pl.ds(index * TAIL_ROWS, TAIL_ROWS)
            for head, part in enumerate((pick(core, own, across), pick(core, across, own))):
                out[:, head, lanes] = part[:PER_BLK]
                out[rows, head, TAIL_AT:] = part[PER_BLK:]


def z_shift(array, by):
    return lax.ppermute(array, "z", [(z, (z + by) % NZ) for z in range(NZ)])


def u_shift(array):
    pairs = []
    for z in range(NZ):
        pairs.append((z * NYLO, ((z + 1) % NZ) * NYLO))
        pairs.append((z * NYLO + 1, ((z - 1) % NZ) * NYLO + 1))
    return lax.ppermute(array, BLK, pairs)


def y_swap(array):
    return lax.ppermute(array, "ylo", [(0, 1), (1, 0)])


def core_swap(array):
    return lax.ppermute(array, "core", [(0, 1), (1, 0)])


def x_turn(array, by):
    return lax.ppermute(array, "x", [(i, (i + by) % NX) for i in range(NX)])


def y_turn(array, by):
    index = lambda y: (y % NYLO) * NYHI + y // NYLO
    pairs = [(index(y), index((y + by) % NY)) for y in range(NY)]
    return lax.ppermute(array, ("ylo", "yhi"), pairs)


def half_swap(array):
    return lax.ppermute(array, "yhi", [(0, 1), (1, 0)])


def body(image_feats, text_feats, image_head, text_head, log_scale, bias):
    image = image_feats[0]
    text = text_feats[0]
    scalars = jnp.concatenate([log_scale, bias])
    block = shape((ROWS, D))
    block32 = shape((ROWS, D), F32)
    column = shape((ROWS, 1), F32)

    text_1 = z_shift(text, 1)
    image_1 = z_shift(image, -1)
    both, raw_u = call(choose_kernel, "choose", [shape((2, ROWS, D)), block], (image, text))
    raw_v0 = y_swap(raw_u)
    packed = call(pack_feats_kernel, "pack_feats", shape((2, ROWS, D)), (both, core_swap(both)))
    feats_1, feats_3 = x_turn(packed, 1), x_turn(packed, 3)
    image_head, text_head = call(
        load_kernel, "load", [shape((D, D)), shape((D, D))], (image_head, text_head),
        in_specs=[HBM_SPEC] * 2, scratch=[pltpu.SemaphoreType.DMA((2,))], mib=46,
    )
    image_1, text_1, packed = lax.optimization_barrier((image_1, text_1, packed))
    u1, v1 = call(
        project_came_kernel, "project_came", [block, block],
        (image_1, text_1, image_head, text_head),
    )
    u2 = y_swap(v1)
    raw_v0, both, u1 = lax.optimization_barrier((raw_v0, both, u1))
    u, v, unit_u, unit_v, norm_u, norm_v = call(
        project_kernel, "project", [block, block, block32, block32, column, column],
        (both, image_head, text_head),
    )
    grad_u, grad_v = call(
        early_kernel, "early", [block32, block32],
        (scalars, u, v, u1, v1, raw_v0, image_head, text_head),
        in_specs=[SMEM_SPEC] + [VMEM_SPEC] * 7,
        scratch=[pltpu.VMEM((ROWS, D), BF16)],
    )
    u2, u1, grad_u, grad_v, feats_1, feats_3 = lax.optimization_barrier(
        (u2, u1, grad_u, grad_v, feats_1, feats_3)
    )
    u3 = u_shift(u2)
    v3 = y_swap(u1)
    feats_2 = (x_turn(feats_1[0], 1), x_turn(feats_3[1], 3))
    grad_v = call(
        middle_kernel, "middle", block32, (scalars, v, u2, grad_v),
        in_specs=[SMEM_SPEC] + [VMEM_SPEC] * 3,
    )
    sent = shape((2, SENT, ROWS))
    image_dpre, text_dpre, *parts = call(
        late_kernel, "late", [block, block, sent, sent, sent, sent],
        (scalars, u, v, u3, v3, grad_u, grad_v, unit_u, unit_v, norm_u, norm_v),
        in_specs=[SMEM_SPEC] + [VMEM_SPEC] * 10,
        scratch=[pltpu.VMEM((D, ROWS), BF16)] * 2,
    )
    image_dpre, text_dpre, feats_2 = lax.optimization_barrier((image_dpre, text_dpre, feats_2))
    image_out, text_out = call(
        feats_grad_kernel, "feats_grad", [block, block],
        (image_dpre, text_dpre, image_head, text_head),
    )
    feats_own, feats_across = call(
        turn_kernel, "turn", [shape((D, NX * ROWS))] * 2, (packed, feats_1, feats_3, *feats_2)
    )
    came = [x_turn(parts[1], 1), x_turn(parts[3], 3), x_turn(parts[2], 2)]
    came, image_out, text_out, feats_own, feats_across = lax.optimization_barrier(
        (came, image_out, text_out, feats_own, feats_across)
    )
    parts = [parts[0]] + came
    others = call(others_kernel, "others", shape((NX, SENT, ROWS)), parts)
    across = core_swap(others)
    own_head = call(
        own_head_kernel, "own_head", shape((D, SENT), F32), [feats_own] + parts,
        scratch=[pltpu.VMEM((SENT, NX * ROWS), BF16)],
    )
    pieces = call(
        head_kernel, "head", [shape((NZ, PIECE, LANES))] * NY, (feats_across, across, own_head),
        scratch=[
            pltpu.VMEM((SENT, NX * ROWS), BF16),
            pltpu.VMEM((D, SENT), F32),
            pltpu.VMEM((D, LANES), F32),
        ],
    )
    pieces = [pieces[0]] + [y_turn(pieces[by], by) for by in (2, 1, 3)]
    pieces = call(add_kernel, "add_y", shape((NZ, PIECE, LANES)), pieces)
    pieces = lax.all_to_all(pieces, "z", 0, 0, tiled=True)
    mine = call(add_z_kernel, "add_z", shape((PIECE, LANES)), (pieces,))
    two = jnp.stack([mine, half_swap(mine)])
    eight = jnp.stack([two] + [x_turn(two, by) for by in range(1, NX)])
    places = (eight, core_swap(eight))
    head_grads = call(place_kernel, "place", shape((PER_BLK, 2, D), F32), places)
    return (image_out[None], text_out[None], head_grads)


def solution(mesh):
    split = Mesh(mesh.devices.reshape(NZ, NYLO, NYHI, NX, NCORE), BLK + REP)
    rows = P(REP, BLK, None)
    return jax.shard_map(
        body,
        mesh=split,
        in_specs=(rows, rows, P(), P(), P(), P()),
        out_specs=(rows, rows, P(BLK, None, None)),
        check_vma=False,
    )
```

```python
import functools

import jax
import jax.numpy as jnp
from jax import lax
from jax.experimental import pallas as pl
from jax.experimental.pallas import tpu as pltpu
from jax.sharding import Mesh
from jax.sharding import PartitionSpec as P

EPSILON = 1e-06
F32 = jnp.float32
BF16 = jnp.bfloat16

BLK = ("z", "ylo")
REP = ("yhi", "x", "core")
NZ, NYLO, NYHI, NX, NCORE = 8, 2, 2, 4, 2
D = 1152
ROWS = 128
LANES = 128
MAIN = 2 * LANES
TAIL_AT = NX * MAIN
SENT = MAIN + LANES
PER_BLK = D // (NZ * NYLO)
TAIL_ROWS = PER_BLK // (NX * NYHI)
PIECE = PER_BLK + TAIL_ROWS
NY = NYLO * NYHI
MIB = 1024 * 1024


def call(kernel, name, out_shape, args, in_specs=None, scratch=(), mib=24):
    return pl.pallas_call(
        kernel,
        out_shape=out_shape,
        in_specs=in_specs or [pl.BlockSpec(memory_space=pltpu.VMEM)] * len(args),
        scratch_shapes=list(scratch),
        compiler_params=pltpu.CompilerParams(vmem_limit_bytes=mib * MIB),
        cost_estimate=pl.CostEstimate(flops=1, bytes_accessed=1, transcendentals=0),
        name=name,
    )(*args)


def shape(dims, dtype=BF16):
    return jax.ShapeDtypeStruct(dims, dtype)


VMEM_SPEC = pl.BlockSpec(memory_space=pltpu.VMEM)
HBM_SPEC = pl.BlockSpec(memory_space=pltpu.HBM)
SMEM_SPEC = pl.BlockSpec(memory_space=pltpu.SMEM)


def nt(left, right):
    return lax.dot_general(left, right, (((1,), (1,)), ((), ())), preferred_element_type=F32)


def nn(left, right):
    return lax.dot_general(left, right, (((1,), (0,)), ((), ())), preferred_element_type=F32)


def pick(flag, if_zero, if_one):
    return jnp.where(flag == 0, if_zero, if_one)


def project(rows, head):
    pre = nn(rows, head[...])
    norm = jnp.sqrt(jnp.sum(pre * pre, axis=1, keepdims=True) + EPSILON)
    return pre / norm, norm


def choose_kernel(image, text, both, raw_u):
    core = lax.axis_index("core")
    both[0] = pick(core, image[...], text[...])
    both[1] = pick(core, text[...], image[...])
    raw_u[...] = pick(lax.axis_index("ylo"), text[...], image[...])


def pack_feats_kernel(both, across, packed):
    packed[0] = both[0]
    packed[1] = across[1]


def load_kernel(image_head_hbm, text_head_hbm, image_head, text_head, sems):
    copies = [
        pltpu.make_async_copy(image_head_hbm, image_head, sems.at[0]),
        pltpu.make_async_copy(text_head_hbm, text_head, sems.at[1]),
    ]
    for copy in copies:
        copy.start()
    for copy in copies:
        copy.wait()


def project_kernel(
    scalars, both, image_head, text_head, emb_u, emb_v, unit_u, unit_v, norm_u, norm_v, pair_scalars
):
    col = lax.axis_index("ylo")
    core = lax.axis_index("core")
    pair_scalars[:4] = jnp.exp(jnp.full((4, LANES), scalars[0], F32))
    pair_scalars[4:] = jnp.full((4, LANES), scalars[1], F32)
    image_unit, image_norm = project(pick(core, both[0], both[1]), image_head)
    text_unit, text_norm = project(pick(core, both[1], both[0]), text_head)
    u = pick(col, text_unit, image_unit)
    v = pick(col, image_unit, text_unit)
    emb_u[...] = u.astype(BF16)
    emb_v[...] = v.astype(BF16)
    unit_u[...] = u
    unit_v[...] = v
    norm_u[...] = pick(col, text_norm, image_norm)
    norm_v[...] = pick(col, image_norm, text_norm)


def project_came_kernel(kind, image, text, image_head, text_head, emb):
    images = lax.axis_index("ylo") == kind

    @pl.when(images)
    def _():
        emb[...] = project(image[...], image_head)[0].astype(BF16)

    @pl.when(jnp.logical_not(images))
    def _():
        emb[...] = project(text[...], text_head)[0].astype(BF16)


def turn_kernel(*refs):
    parts, turned = refs[:-2], refs[-2:]
    blocks = [part[side] for part in parts[:-2] for side in range(NCORE)]
    blocks += [part[...] for part in parts[-2:]]
    for place, rows in enumerate(blocks):
        step, side = divmod(place, NCORE)
        turned[side][:, step * ROWS:(step + 1) * ROWS] = rows.astype(F32).T.astype(BF16)


def pair_weights(own, other, scalars, same):
    scale = scalars[:1]
    logits = scale * nt(own, other) + scalars[4:5]
    probs = jax.nn.sigmoid(logits)
    if same:
        row = lax.broadcasted_iota(jnp.int32, probs.shape, 0)
        column = lax.broadcasted_iota(jnp.int32, probs.shape, 1)
        probs = probs - jnp.where(row == column, 1.0, 0.0)
    return (scale * probs).astype(BF16)


def pull(own, other, scalars, same=False):
    return nn(pair_weights(own, other, scalars, same), other)


def early_kernel(scalars, u, v, u1, v1, raw_v0, image_head, text_head, grad_u, grad_v, emb_v0):
    col = lax.axis_index("ylo")

    @pl.when(col == 0)
    def _():
        emb_v0[...] = project(raw_v0[...], image_head)[0].astype(BF16)

    @pl.when(col == 1)
    def _():
        emb_v0[...] = project(raw_v0[...], text_head)[0].astype(BF16)

    own_u, own_v = u[...], v[...]
    grad_u[...] = (
        pull(own_u, own_v, scalars, True)
        + pull(own_u, v1[...], scalars)
        + pull(own_u, emb_v0[...], scalars)
    )
    grad_v[...] = pull(own_v, own_u, scalars, True) + pull(own_v, u1[...], scalars)


def middle_kernel(scalars, v, u2, grad_v, out):
    out[...] = grad_v[...] + pull(v[...], u2[...], scalars)


def late_kernel(
    scalars, u, v, u3, v3, grad_u, grad_v, unit_u, unit_v, norm_u, norm_v,
    image_dpre, text_dpre, sent0, sent1, sent2, sent3, mine_t, other_t,
):
    col = lax.axis_index("ylo")
    core = lax.axis_index("core")
    at = lax.axis_index("x")

    def backward(grad, unit, norm):
        radial = jnp.sum(unit * grad, axis=1, keepdims=True)
        return (grad - unit * radial) / norm

    dpre_u = backward(grad_u[...] + pull(u[...], v3[...], scalars), unit_u[...], norm_u[...])
    dpre_v = backward(grad_v[...] + pull(v[...], u3[...], scalars), unit_v[...], norm_v[...])
    image = pick(col, dpre_v, dpre_u)
    text = pick(col, dpre_u, dpre_v)
    image_dpre[...] = image.astype(BF16)
    text_dpre[...] = text.astype(BF16)
    mine_t[...] = pick(core, image, text).T.astype(BF16)
    other_t[...] = pick(core, text, image).T.astype(BF16)
    for step, sent in enumerate((sent0, sent1, sent2, sent3)):
        to = lax.rem(at + step, NX)
        rows = pl.ds(pl.multiple_of(to * MAIN, MAIN), MAIN)
        for place, turned in enumerate((mine_t, other_t)):
            sent[place, :MAIN, :] = turned[rows, :]
            sent[place, MAIN:, :] = turned[TAIL_AT:, :]


def others_kernel(*refs):
    parts, others = refs[:-1], refs[-1]
    for step, part in enumerate(parts):
        others[step] = part[1]


def feats_grad_kernel(image_dpre, text_dpre, image_head, text_head, image_out, text_out):
    image_out[...] = nt(image_dpre[...], image_head[...]).astype(BF16)
    text_out[...] = nt(text_dpre[...], text_head[...]).astype(BF16)


def own_head_kernel(feats_t, *refs):
    parts, total, right = refs[:NX], refs[NX], refs[NX + 1]
    for place, part in enumerate(parts):
        right[:, place * ROWS:(place + 1) * ROWS] = part[0]
    total[...] = nt(feats_t[...], right[...])


def head_kernel(feats_t, across, own, *refs):
    pieces, right, total, tails = refs[:NY], *refs[NY:]
    at = lax.axis_index("x")
    y = NYLO * lax.axis_index("yhi") + lax.axis_index("ylo")
    for place in range(NX):
        right[:, place * ROWS:(place + 1) * ROWS] = across[place]
    total[...] = own[...] + nt(feats_t[...], right[...])
    tails[...] = total[:, MAIN:]
    for step, piece in enumerate(pieces):
        to = lax.rem(y + step, NY)
        half, low = to // NYLO, lax.rem(to, NYLO)
        lanes = pl.ds(pl.multiple_of(half * LANES, LANES), LANES)
        for z in range(NZ):
            start = pl.multiple_of((z * NYLO + low) * PER_BLK, 8)
            tail = start + (NYHI * at + half) * TAIL_ROWS
            rows = [
                total[pl.ds(start, PER_BLK), lanes],
                tails[pl.ds(tail, TAIL_ROWS), :],
            ]
            piece[z] = jnp.concatenate(rows, axis=0).astype(BF16)


def add_kernel(*refs):
    parts, out = refs[:-1], refs[-1]
    total = parts[0][...].astype(F32)
    for part in parts[1:]:
        total = total + part[...].astype(F32)
    out[...] = total.astype(BF16)


def add_z_kernel(pieces, out):
    total = pieces[0].astype(F32)
    for place in range(1, NZ):
        total = total + pieces[place].astype(F32)
    out[...] = total.astype(BF16)


def place_kernel(mine, other, out):
    core = lax.axis_index("core")
    at = lax.axis_index("x")
    half_at = lax.axis_index("yhi")
    for step in range(NX):
        came_x = lax.rem(at + NX - step, NX)
        for flip in range(NYHI):
            index = NYHI * came_x + lax.rem(half_at + flip, NYHI)
            own = mine[step, flip].astype(F32)
            across = other[step, flip].astype(F32)
            lanes = pl.ds(pl.multiple_of(index * LANES, LANES), LANES)
            rows = pl.ds(index * TAIL_ROWS, TAIL_ROWS)
            for head, part in enumerate((pick(core, own, across), pick(core, across, own))):
                out[:, head, lanes] = part[:PER_BLK]
                out[rows, head, TAIL_AT:] = part[PER_BLK:]


def z_shift(array, by):
    return lax.ppermute(array, "z", [(z, (z + by) % NZ) for z in range(NZ)])


def u_shift(array):
    pairs = []
    for z in range(NZ):
        pairs.append((z * NYLO, ((z + 1) % NZ) * NYLO))
        pairs.append((z * NYLO + 1, ((z - 1) % NZ) * NYLO + 1))
    return lax.ppermute(array, BLK, pairs)


def y_swap(array):
    return lax.ppermute(array, "ylo", [(0, 1), (1, 0)])


def core_swap(array):
    return lax.ppermute(array, "core", [(0, 1), (1, 0)])


def x_turn(array, by):
    return lax.ppermute(array, "x", [(i, (i + by) % NX) for i in range(NX)])


def y_turn(array, by):
    index = lambda y: (y % NYLO) * NYHI + y // NYLO
    pairs = [(index(y), index((y + by) % NY)) for y in range(NY)]
    return lax.ppermute(array, ("ylo", "yhi"), pairs)


def half_swap(array):
    return lax.ppermute(array, "yhi", [(0, 1), (1, 0)])


def body(image_feats, text_feats, image_head, text_head, log_scale, bias):
    image = image_feats[0]
    text = text_feats[0]
    scalars = jnp.concatenate([log_scale, bias])
    block = shape((ROWS, D))
    block32 = shape((ROWS, D), F32)
    column = shape((ROWS, 1), F32)

    text_1 = z_shift(text, 1)
    image_1 = z_shift(image, -1)
    both, raw_u = call(choose_kernel, "choose", [shape((2, ROWS, D)), block], (image, text))
    raw_v0 = y_swap(raw_u)
    packed = call(pack_feats_kernel, "pack_feats", shape((2, ROWS, D)), (both, core_swap(both)))
    feats_1, feats_3 = x_turn(packed, 1), x_turn(packed, 3)
    image_head, text_head = call(
        load_kernel, "load", [shape((D, D)), shape((D, D))], (image_head, text_head),
        in_specs=[HBM_SPEC] * 2, scratch=[pltpu.SemaphoreType.DMA((2,))], mib=46,
    )
    image_1, text_1, packed = lax.optimization_barrier((image_1, text_1, packed))
    came = (image_1, text_1, image_head, text_head)
    v1 = call(functools.partial(project_came_kernel, 0), "project_v", block, came)
    u2 = y_swap(v1)
    raw_v0, both, image_1, text_1, v1 = lax.optimization_barrier(
        (raw_v0, both, image_1, text_1, v1)
    )
    came = (image_1, text_1, image_head, text_head)
    u1 = call(functools.partial(project_came_kernel, 1), "project_u", block, came)
    u, v, unit_u, unit_v, norm_u, norm_v, scalars = call(
        project_kernel, "project",
        [block, block, block32, block32, column, column, shape((8, LANES), F32)],
        (scalars, both, image_head, text_head), in_specs=[SMEM_SPEC] + [VMEM_SPEC] * 3,
    )
    grad_u, grad_v = call(
        early_kernel, "early", [block32, block32],
        (scalars, u, v, u1, v1, raw_v0, image_head, text_head),
        scratch=[pltpu.VMEM((ROWS, D), BF16)],
    )
    u2, u1, grad_u, grad_v, feats_1, feats_3 = lax.optimization_barrier(
        (u2, u1, grad_u, grad_v, feats_1, feats_3)
    )
    u3 = u_shift(u2)
    v3 = y_swap(u1)
    feats_2 = (x_turn(feats_1[0], 1), x_turn(feats_3[1], 3))
    grad_v = call(
        middle_kernel, "middle", block32, (scalars, v, u2, grad_v)
    )
    sent = shape((2, SENT, ROWS))
    image_dpre, text_dpre, *parts = call(
        late_kernel, "late", [block, block, sent, sent, sent, sent],
        (scalars, u, v, u3, v3, grad_u, grad_v, unit_u, unit_v, norm_u, norm_v),
        scratch=[pltpu.VMEM((D, ROWS), BF16)] * 2,
    )
    image_dpre, text_dpre, feats_2 = lax.optimization_barrier((image_dpre, text_dpre, feats_2))
    image_out, text_out = call(
        feats_grad_kernel, "feats_grad", [block, block],
        (image_dpre, text_dpre, image_head, text_head),
    )
    feats_own, feats_across = call(
        turn_kernel, "turn", [shape((D, NX * ROWS))] * 2, (packed, feats_1, feats_3, *feats_2)
    )
    came = [x_turn(parts[1], 1), x_turn(parts[3], 3), x_turn(parts[2], 2)]
    came, image_out, text_out, feats_own, feats_across = lax.optimization_barrier(
        (came, image_out, text_out, feats_own, feats_across)
    )
    parts = [parts[0]] + came
    others = call(others_kernel, "others", shape((NX, SENT, ROWS)), parts)
    across = core_swap(others)
    own_head = call(
        own_head_kernel, "own_head", shape((D, SENT), F32), [feats_own] + parts,
        scratch=[pltpu.VMEM((SENT, NX * ROWS), BF16)],
    )
    pieces = call(
        head_kernel, "head", [shape((NZ, PIECE, LANES))] * NY, (feats_across, across, own_head),
        scratch=[
            pltpu.VMEM((SENT, NX * ROWS), BF16),
            pltpu.VMEM((D, SENT), F32),
            pltpu.VMEM((D, LANES), F32),
        ],
    )
    pieces = [pieces[0]] + [y_turn(pieces[by], by) for by in (2, 1, 3)]
    pieces = call(add_kernel, "add_y", shape((NZ, PIECE, LANES)), pieces)
    pieces = lax.all_to_all(pieces, "z", 0, 0, tiled=True)
    mine = call(add_z_kernel, "add_z", shape((PIECE, LANES)), (pieces,))
    two = jnp.stack([mine, half_swap(mine)])
    eight = jnp.stack([two] + [x_turn(two, by) for by in range(1, NX)])
    places = (eight, core_swap(eight))
    head_grads = call(place_kernel, "place", shape((PER_BLK, 2, D), F32), places)
    return (image_out[None], text_out[None], head_grads)


def solution(mesh):
    split = Mesh(mesh.devices.reshape(NZ, NYLO, NYHI, NX, NCORE), BLK + REP)
    rows = P(REP, BLK, None)
    return jax.shard_map(
        body,
        mesh=split,
        in_specs=(rows, rows, P(), P(), P(), P()),
        out_specs=(rows, rows, P(BLK, None, None)),
        check_vma=False,
    )
```

```python
import functools

import jax
import jax.numpy as jnp
from jax import lax
from jax.experimental import pallas as pl
from jax.experimental.pallas import tpu as pltpu
from jax.sharding import Mesh
from jax.sharding import PartitionSpec as P

EPSILON = 1e-06
F32 = jnp.float32
BF16 = jnp.bfloat16

BLK = ("z", "ylo")
REP = ("yhi", "x", "core")
NZ, NYLO, NYHI, NX, NCORE = 8, 2, 2, 4, 2
D = 1152
ROWS = 128
LANES = 128
MAIN = 2 * LANES
TAIL_AT = NX * MAIN
SENT = MAIN + LANES
PER_BLK = D // (NZ * NYLO)
TAIL_ROWS = PER_BLK // (NX * NYHI)
PIECE = PER_BLK + TAIL_ROWS
NY = NYLO * NYHI
MIB = 1024 * 1024


def call(kernel, name, out_shape, args, in_specs=None, scratch=(), mib=24):
    return pl.pallas_call(
        kernel,
        out_shape=out_shape,
        in_specs=in_specs or [pl.BlockSpec(memory_space=pltpu.VMEM)] * len(args),
        scratch_shapes=list(scratch),
        compiler_params=pltpu.CompilerParams(vmem_limit_bytes=mib * MIB),
        cost_estimate=pl.CostEstimate(flops=1, bytes_accessed=1, transcendentals=0),
        name=name,
    )(*args)


def shape(dims, dtype=BF16):
    return jax.ShapeDtypeStruct(dims, dtype)


VMEM_SPEC = pl.BlockSpec(memory_space=pltpu.VMEM)
HBM_SPEC = pl.BlockSpec(memory_space=pltpu.HBM)
SMEM_SPEC = pl.BlockSpec(memory_space=pltpu.SMEM)


def nt(left, right):
    return lax.dot_general(left, right, (((1,), (1,)), ((), ())), preferred_element_type=F32)


def nn(left, right):
    return lax.dot_general(left, right, (((1,), (0,)), ((), ())), preferred_element_type=F32)


def pick(flag, if_zero, if_one):
    return jnp.where(flag == 0, if_zero, if_one)


def project(rows, head):
    pre = nn(rows, head[...])
    norm = jnp.sqrt(jnp.sum(pre * pre, axis=1, keepdims=True) + EPSILON)
    return pre / norm, norm


def choose_kernel(image, text, both, raw_u):
    core = lax.axis_index("core")
    both[0] = pick(core, image[...], text[...])
    both[1] = pick(core, text[...], image[...])
    raw_u[...] = pick(lax.axis_index("ylo"), text[...], image[...])


def pack_feats_kernel(both, across, packed):
    packed[0] = both[0]
    packed[1] = across[1]


def load_kernel(image_head_hbm, text_head_hbm, image_head, text_head, sems):
    copies = [
        pltpu.make_async_copy(image_head_hbm, image_head, sems.at[0]),
        pltpu.make_async_copy(text_head_hbm, text_head, sems.at[1]),
    ]
    for copy in copies:
        copy.start()
    for copy in copies:
        copy.wait()


def project_kernel(
    scalars, both, image_head, text_head, emb_u, emb_v, unit_u, unit_v, norm_u, norm_v, pair_scalars
):
    col = lax.axis_index("ylo")
    core = lax.axis_index("core")
    pair_scalars[:4] = jnp.exp(jnp.full((4, LANES), scalars[0], F32))
    pair_scalars[4:] = jnp.full((4, LANES), scalars[1], F32)
    image_unit, image_norm = project(pick(core, both[0], both[1]), image_head)
    text_unit, text_norm = project(pick(core, both[1], both[0]), text_head)
    u = pick(col, text_unit, image_unit)
    v = pick(col, image_unit, text_unit)
    emb_u[...] = u.astype(BF16)
    emb_v[...] = v.astype(BF16)
    unit_u[...] = u
    unit_v[...] = v
    norm_u[...] = pick(col, text_norm, image_norm)
    norm_v[...] = pick(col, image_norm, text_norm)


def project_came_kernel(kind, image, text, image_head, text_head, emb):
    images = lax.axis_index("ylo") == kind

    @pl.when(images)
    def _():
        emb[...] = project(image[...], image_head)[0].astype(BF16)

    @pl.when(jnp.logical_not(images))
    def _():
        emb[...] = project(text[...], text_head)[0].astype(BF16)


def turn_kernel(*refs):
    parts, turned = refs[:-2], refs[-2:]
    blocks = [part[side] for part in parts[:-2] for side in range(NCORE)]
    blocks += [part[...] for part in parts[-2:]]
    for place, rows in enumerate(blocks):
        step, side = divmod(place, NCORE)
        turned[side][:, step * ROWS:(step + 1) * ROWS] = rows.T


def pair_weights(own, other, scalars, same):
    scale = scalars[:1]
    logits = scale * nt(own, other) + scalars[4:5]
    probs = jax.nn.sigmoid(logits)
    if same:
        row = lax.broadcasted_iota(jnp.int32, probs.shape, 0)
        column = lax.broadcasted_iota(jnp.int32, probs.shape, 1)
        probs = probs - jnp.where(row == column, 1.0, 0.0)
    return (scale * probs).astype(BF16)


def pull(own, other, scalars, same=False):
    return nn(pair_weights(own, other, scalars, same), other)


def early_kernel(scalars, u, v, u1, v1, raw_v0, image_head, text_head, grad_u, grad_v, emb_v0):
    col = lax.axis_index("ylo")

    @pl.when(col == 0)
    def _():
        emb_v0[...] = project(raw_v0[...], image_head)[0].astype(BF16)

    @pl.when(col == 1)
    def _():
        emb_v0[...] = project(raw_v0[...], text_head)[0].astype(BF16)

    own_u, own_v = u[...], v[...]
    grad_u[...] = (
        pull(own_u, own_v, scalars, True)
        + pull(own_u, v1[...], scalars)
        + pull(own_u, emb_v0[...], scalars)
    )
    grad_v[...] = pull(own_v, own_u, scalars, True) + pull(own_v, u1[...], scalars)


def middle_kernel(scalars, v, u2, grad_v, out):
    out[...] = grad_v[...] + pull(v[...], u2[...], scalars)


def late_kernel(
    scalars, u, v, u3, v3, grad_u, grad_v, unit_u, unit_v, norm_u, norm_v,
    image_dpre, text_dpre, sent0, sent1, sent2, sent3, mine_t, other_t,
):
    col = lax.axis_index("ylo")
    core = lax.axis_index("core")
    at = lax.axis_index("x")

    def backward(grad, unit, norm):
        radial = jnp.sum(unit * grad, axis=1, keepdims=True)
        return (grad - unit * radial) / norm

    dpre_u = backward(grad_u[...] + pull(u[...], v3[...], scalars), unit_u[...], norm_u[...])
    dpre_v = backward(grad_v[...] + pull(v[...], u3[...], scalars), unit_v[...], norm_v[...])
    image = pick(col, dpre_v, dpre_u)
    text = pick(col, dpre_u, dpre_v)
    image_dpre[...] = image.astype(BF16)
    text_dpre[...] = text.astype(BF16)
    image, text = image.astype(BF16), text.astype(BF16)
    mine_t[...] = pick(core, image, text).T
    other_t[...] = pick(core, text, image).T
    for step, sent in enumerate((sent0, sent1, sent2, sent3)):
        to = lax.rem(at + step, NX)
        rows = pl.ds(pl.multiple_of(to * MAIN, MAIN), MAIN)
        for place, turned in enumerate((mine_t, other_t)):
            sent[place, :MAIN, :] = turned[rows, :]
            sent[place, MAIN:, :] = turned[TAIL_AT:, :]


def others_kernel(*refs):
    parts, others = refs[:-1], refs[-1]
    for step, part in enumerate(parts):
        others[step] = part[1]


def feats_grad_kernel(image_dpre, text_dpre, image_head, text_head, image_out, text_out):
    image_out[...] = nt(image_dpre[...], image_head[...]).astype(BF16)
    text_out[...] = nt(text_dpre[...], text_head[...]).astype(BF16)


def own_head_kernel(feats_t, *refs):
    parts, total, right = refs[:NX], refs[NX], refs[NX + 1]
    for place, part in enumerate(parts):
        right[:, place * ROWS:(place + 1) * ROWS] = part[0]
    total[...] = nt(feats_t[...], right[...])


def head_kernel(feats_t, across, own, *refs):
    pieces, right, total, tails = refs[:NY], *refs[NY:]
    at = lax.axis_index("x")
    y = NYLO * lax.axis_index("yhi") + lax.axis_index("ylo")
    for place in range(NX):
        right[:, place * ROWS:(place + 1) * ROWS] = across[place]
    total[...] = own[...] + nt(feats_t[...], right[...])
    tails[...] = total[:, MAIN:]
    for step, piece in enumerate(pieces):
        to = lax.rem(y + step, NY)
        half, low = to // NYLO, lax.rem(to, NYLO)
        lanes = pl.ds(pl.multiple_of(half * LANES, LANES), LANES)
        for z in range(NZ):
            start = pl.multiple_of((z * NYLO + low) * PER_BLK, 8)
            tail = start + (NYHI * at + half) * TAIL_ROWS
            rows = [
                total[pl.ds(start, PER_BLK), lanes],
                tails[pl.ds(tail, TAIL_ROWS), :],
            ]
            piece[z] = jnp.concatenate(rows, axis=0).astype(BF16)


def add_kernel(*refs):
    parts, out = refs[:-1], refs[-1]
    total = parts[0][...].astype(F32)
    for part in parts[1:]:
        total = total + part[...].astype(F32)
    out[...] = total.astype(BF16)


def add_z_kernel(pieces, out):
    total = pieces[0].astype(F32)
    for place in range(1, NZ):
        total = total + pieces[place].astype(F32)
    out[...] = total.astype(BF16)


def place_kernel(mine, other, out):
    core = lax.axis_index("core")
    at = lax.axis_index("x")
    half_at = lax.axis_index("yhi")
    for step in range(NX):
        came_x = lax.rem(at + NX - step, NX)
        for flip in range(NYHI):
            index = NYHI * came_x + lax.rem(half_at + flip, NYHI)
            own = mine[step, flip]
            across = other[step, flip]
            lanes = pl.ds(pl.multiple_of(index * LANES, LANES), LANES)
            rows = pl.ds(index * TAIL_ROWS, TAIL_ROWS)
            for head, part in enumerate((pick(core, own, across), pick(core, across, own))):
                part = part.astype(F32)
                out[:, head, lanes] = part[:PER_BLK]
                out[rows, head, TAIL_AT:] = part[PER_BLK:]


def z_shift(array, by):
    return lax.ppermute(array, "z", [(z, (z + by) % NZ) for z in range(NZ)])


def u_shift(array):
    pairs = []
    for z in range(NZ):
        pairs.append((z * NYLO, ((z + 1) % NZ) * NYLO))
        pairs.append((z * NYLO + 1, ((z - 1) % NZ) * NYLO + 1))
    return lax.ppermute(array, BLK, pairs)


def y_swap(array):
    return lax.ppermute(array, "ylo", [(0, 1), (1, 0)])


def core_swap(array):
    return lax.ppermute(array, "core", [(0, 1), (1, 0)])


def x_turn(array, by):
    return lax.ppermute(array, "x", [(i, (i + by) % NX) for i in range(NX)])


def y_turn(array, by):
    index = lambda y: (y % NYLO) * NYHI + y // NYLO
    pairs = [(index(y), index((y + by) % NY)) for y in range(NY)]
    return lax.ppermute(array, ("ylo", "yhi"), pairs)


def half_swap(array):
    return lax.ppermute(array, "yhi", [(0, 1), (1, 0)])


def body(image_feats, text_feats, image_head, text_head, log_scale, bias):
    image = image_feats[0]
    text = text_feats[0]
    scalars = jnp.concatenate([log_scale, bias])
    block = shape((ROWS, D))
    block32 = shape((ROWS, D), F32)
    column = shape((ROWS, 1), F32)

    text_1 = z_shift(text, 1)
    image_1 = z_shift(image, -1)
    both, raw_u = call(choose_kernel, "choose", [shape((2, ROWS, D)), block], (image, text))
    raw_v0 = y_swap(raw_u)
    packed = call(pack_feats_kernel, "pack_feats", shape((2, ROWS, D)), (both, core_swap(both)))
    feats_1, feats_3 = x_turn(packed, 1), x_turn(packed, 3)
    image_head, text_head = call(
        load_kernel, "load", [shape((D, D)), shape((D, D))], (image_head, text_head),
        in_specs=[HBM_SPEC] * 2, scratch=[pltpu.SemaphoreType.DMA((2,))], mib=46,
    )
    image_1, text_1, packed = lax.optimization_barrier((image_1, text_1, packed))
    came = (image_1, text_1, image_head, text_head)
    v1 = call(functools.partial(project_came_kernel, 0), "project_v", block, came)
    u2 = y_swap(v1)
    raw_v0, both, image_1, text_1, v1 = lax.optimization_barrier(
        (raw_v0, both, image_1, text_1, v1)
    )
    came = (image_1, text_1, image_head, text_head)
    u1 = call(functools.partial(project_came_kernel, 1), "project_u", block, came)
    u, v, unit_u, unit_v, norm_u, norm_v, scalars = call(
        project_kernel, "project",
        [block, block, block32, block32, column, column, shape((8, LANES), F32)],
        (scalars, both, image_head, text_head), in_specs=[SMEM_SPEC] + [VMEM_SPEC] * 3,
    )
    grad_u, grad_v = call(
        early_kernel, "early", [block32, block32],
        (scalars, u, v, u1, v1, raw_v0, image_head, text_head),
        scratch=[pltpu.VMEM((ROWS, D), BF16)],
    )
    u2, u1, grad_u, grad_v, feats_1, feats_3 = lax.optimization_barrier(
        (u2, u1, grad_u, grad_v, feats_1, feats_3)
    )
    u3 = u_shift(u2)
    v3 = y_swap(u1)
    feats_2 = (x_turn(feats_1[0], 1), x_turn(feats_3[1], 3))
    grad_v = call(
        middle_kernel, "middle", block32, (scalars, v, u2, grad_v)
    )
    sent = shape((2, SENT, ROWS))
    image_dpre, text_dpre, *parts = call(
        late_kernel, "late", [block, block, sent, sent, sent, sent],
        (scalars, u, v, u3, v3, grad_u, grad_v, unit_u, unit_v, norm_u, norm_v),
        scratch=[pltpu.VMEM((D, ROWS), BF16)] * 2,
    )
    image_dpre, text_dpre, feats_2 = lax.optimization_barrier((image_dpre, text_dpre, feats_2))
    image_out, text_out = call(
        feats_grad_kernel, "feats_grad", [block, block],
        (image_dpre, text_dpre, image_head, text_head),
    )
    feats_own, feats_across = call(
        turn_kernel, "turn", [shape((D, NX * ROWS))] * 2, (packed, feats_1, feats_3, *feats_2)
    )
    far = x_turn(parts[2], 2)
    came = [x_turn(parts[1], 1), x_turn(parts[3], 3), far]
    came, image_out, text_out, feats_own, feats_across = lax.optimization_barrier(
        (came, image_out, text_out, feats_own, feats_across)
    )
    parts = [parts[0]] + came
    others = call(others_kernel, "others", shape((NX, SENT, ROWS)), parts)
    across = core_swap(others)
    own_head = call(
        own_head_kernel, "own_head", shape((D, SENT), F32), [feats_own] + parts,
        scratch=[pltpu.VMEM((SENT, NX * ROWS), BF16)],
    )
    pieces = call(
        head_kernel, "head", [shape((NZ, PIECE, LANES))] * NY, (feats_across, across, own_head),
        scratch=[
            pltpu.VMEM((SENT, NX * ROWS), BF16),
            pltpu.VMEM((D, SENT), F32),
            pltpu.VMEM((D, LANES), F32),
        ],
    )
    pieces = [pieces[0]] + [y_turn(pieces[by], by) for by in (2, 1, 3)]
    pieces = call(add_kernel, "add_y", shape((NZ, PIECE, LANES)), pieces)
    pieces = lax.all_to_all(pieces, "z", 0, 0, tiled=True)
    mine = call(add_z_kernel, "add_z", shape((PIECE, LANES)), (pieces,))
    two = jnp.stack([mine, half_swap(mine)])
    far = x_turn(two, 2)
    eight = jnp.stack([two, x_turn(two, 1), far, x_turn(two, 3)])
    places = (eight, core_swap(eight))
    head_grads = call(place_kernel, "place", shape((PER_BLK, 2, D), F32), places)
    return (image_out[None], text_out[None], head_grads)


def solution(mesh):
    split = Mesh(mesh.devices.reshape(NZ, NYLO, NYHI, NX, NCORE), BLK + REP)
    rows = P(REP, BLK, None)
    return jax.shard_map(
        body,
        mesh=split,
        in_specs=(rows, rows, P(), P(), P(), P()),
        out_specs=(rows, rows, P(BLK, None, None)),
        check_vma=False,
    )
```

```python
import functools

import jax
import jax.numpy as jnp
from jax import lax
from jax.experimental import pallas as pl
from jax.experimental.pallas import tpu as pltpu
from jax.sharding import Mesh
from jax.sharding import PartitionSpec as P

EPSILON = 1e-06
F32 = jnp.float32
BF16 = jnp.bfloat16

BLK = ("z", "ylo")
REP = ("yhi", "x", "core")
NZ, NYLO, NYHI, NX, NCORE = 8, 2, 2, 4, 2
D = 1152
ROWS = 128
LANES = 128
MAIN = 2 * LANES
TAIL_AT = NX * MAIN
SENT = MAIN + LANES
PER_BLK = D // (NZ * NYLO)
TAIL_ROWS = PER_BLK // (NX * NYHI)
PIECE = PER_BLK + TAIL_ROWS
NY = NYLO * NYHI
MIB = 1024 * 1024


def call(kernel, name, out_shape, args, in_specs=None, scratch=(), mib=24):
    return pl.pallas_call(
        kernel,
        out_shape=out_shape,
        in_specs=in_specs or [pl.BlockSpec(memory_space=pltpu.VMEM)] * len(args),
        scratch_shapes=list(scratch),
        compiler_params=pltpu.CompilerParams(vmem_limit_bytes=mib * MIB),
        cost_estimate=pl.CostEstimate(flops=1, bytes_accessed=1, transcendentals=0),
        name=name,
    )(*args)


def shape(dims, dtype=BF16):
    return jax.ShapeDtypeStruct(dims, dtype)


VMEM_SPEC = pl.BlockSpec(memory_space=pltpu.VMEM)
SMEM_SPEC = pl.BlockSpec(memory_space=pltpu.SMEM)


def nt(left, right):
    return lax.dot_general(left, right, (((1,), (1,)), ((), ())), preferred_element_type=F32)


def nn(left, right):
    return lax.dot_general(left, right, (((1,), (0,)), ((), ())), preferred_element_type=F32)


def pick(flag, if_zero, if_one):
    return jnp.where(flag == 0, if_zero, if_one)


def project(rows, head):
    pre = nn(rows, head[...])
    norm = jnp.sqrt(jnp.sum(pre * pre, axis=1, keepdims=True) + EPSILON)
    return pre / norm, norm


def choose_kernel(image, text, both, raw_u):
    core = lax.axis_index("core")
    both[0] = pick(core, image[...], text[...])
    both[1] = pick(core, text[...], image[...])
    raw_u[...] = pick(lax.axis_index("ylo"), text[...], image[...])


def pack_feats_kernel(both, across, packed):
    packed[0] = both[0]
    packed[1] = across[1]


def project_kernel(
    scalars, both, image_head, text_head, emb_u, emb_v, unit_u, unit_v, norm_u, norm_v, pair_scalars
):
    col = lax.axis_index("ylo")
    core = lax.axis_index("core")
    pair_scalars[:4] = jnp.exp(jnp.full((4, LANES), scalars[0], F32))
    pair_scalars[4:] = jnp.full((4, LANES), scalars[1], F32)
    image_unit, image_norm = project(pick(core, both[0], both[1]), image_head)
    text_unit, text_norm = project(pick(core, both[1], both[0]), text_head)
    u = pick(col, text_unit, image_unit)
    v = pick(col, image_unit, text_unit)
    emb_u[...] = u.astype(BF16)
    emb_v[...] = v.astype(BF16)
    unit_u[...] = u
    unit_v[...] = v
    norm_u[...] = pick(col, text_norm, image_norm)
    norm_v[...] = pick(col, image_norm, text_norm)


def project_came_kernel(kind, image, text, image_head, text_head, emb):
    images = lax.axis_index("ylo") == kind

    @pl.when(images)
    def _():
        emb[...] = project(image[...], image_head)[0].astype(BF16)

    @pl.when(jnp.logical_not(images))
    def _():
        emb[...] = project(text[...], text_head)[0].astype(BF16)


def turn_kernel(*refs):
    parts, turned = refs[:-2], refs[-2:]
    blocks = [part[side] for part in parts[:-2] for side in range(NCORE)]
    blocks += [part[...] for part in parts[-2:]]
    for place, rows in enumerate(blocks):
        step, side = divmod(place, NCORE)
        turned[side][:, step * ROWS:(step + 1) * ROWS] = rows.T


def pair_weights(own, other, scalars, same):
    scale = scalars[:1]
    logits = scale * nt(own, other) + scalars[4:5]
    probs = jax.nn.sigmoid(logits)
    if same:
        row = lax.broadcasted_iota(jnp.int32, probs.shape, 0)
        column = lax.broadcasted_iota(jnp.int32, probs.shape, 1)
        probs = probs - jnp.where(row == column, 1.0, 0.0)
    return (scale * probs).astype(BF16)


def pull(own, other, scalars, same=False):
    return nn(pair_weights(own, other, scalars, same), other)


def early_kernel(scalars, u, v, u1, v1, raw_v0, image_head, text_head, grad_u, grad_v, emb_v0):
    col = lax.axis_index("ylo")

    @pl.when(col == 0)
    def _():
        emb_v0[...] = project(raw_v0[...], image_head)[0].astype(BF16)

    @pl.when(col == 1)
    def _():
        emb_v0[...] = project(raw_v0[...], text_head)[0].astype(BF16)

    own_u, own_v = u[...], v[...]
    grad_u[...] = (
        pull(own_u, own_v, scalars, True)
        + pull(own_u, v1[...], scalars)
        + pull(own_u, emb_v0[...], scalars)
    )
    grad_v[...] = pull(own_v, own_u, scalars, True) + pull(own_v, u1[...], scalars)


def middle_kernel(scalars, v, u2, grad_v, out):
    out[...] = grad_v[...] + pull(v[...], u2[...], scalars)


def late_kernel(
    scalars, u, v, u3, v3, grad_u, grad_v, unit_u, unit_v, norm_u, norm_v,
    image_dpre, text_dpre, sent0, sent1, sent2, sent3, mine_t, other_t,
):
    col = lax.axis_index("ylo")
    core = lax.axis_index("core")
    at = lax.axis_index("x")

    def backward(grad, unit, norm):
        radial = jnp.sum(unit * grad, axis=1, keepdims=True)
        return (grad - unit * radial) / norm

    dpre_u = backward(grad_u[...] + pull(u[...], v3[...], scalars), unit_u[...], norm_u[...])
    dpre_v = backward(grad_v[...] + pull(v[...], u3[...], scalars), unit_v[...], norm_v[...])
    image = pick(col, dpre_v, dpre_u)
    text = pick(col, dpre_u, dpre_v)
    image_dpre[...] = image.astype(BF16)
    text_dpre[...] = text.astype(BF16)
    image, text = image.astype(BF16), text.astype(BF16)
    mine_t[...] = pick(core, image, text).T
    other_t[...] = pick(core, text, image).T
    for step, sent in enumerate((sent0, sent1, sent2, sent3)):
        to = lax.rem(at + step, NX)
        rows = pl.ds(pl.multiple_of(to * MAIN, MAIN), MAIN)
        for place, turned in enumerate((mine_t, other_t)):
            sent[place, :MAIN, :] = turned[rows, :]
            sent[place, MAIN:, :] = turned[TAIL_AT:, :]


def others_kernel(*refs):
    parts, others = refs[:-1], refs[-1]
    for step, part in enumerate(parts):
        others[step] = part[1]


def feats_grad_kernel(image_dpre, text_dpre, image_head, text_head, image_out, text_out):
    image_out[...] = nt(image_dpre[...], image_head[...]).astype(BF16)
    text_out[...] = nt(text_dpre[...], text_head[...]).astype(BF16)


def own_head_kernel(feats_t, *refs):
    parts, total, right = refs[:NX], refs[NX], refs[NX + 1]
    for place, part in enumerate(parts):
        right[:, place * ROWS:(place + 1) * ROWS] = part[0]
    total[...] = nt(feats_t[...], right[...])


def head_kernel(feats_t, across, own, *refs):
    pieces, right, total, tails = refs[:NY], *refs[NY:]
    at = lax.axis_index("x")
    y = NYLO * lax.axis_index("yhi") + lax.axis_index("ylo")
    for place in range(NX):
        right[:, place * ROWS:(place + 1) * ROWS] = across[place]
    total[...] = own[...] + nt(feats_t[...], right[...])
    tails[...] = total[:, MAIN:]
    for step, piece in enumerate(pieces):
        to = lax.rem(y + step, NY)
        half, low = to // NYLO, lax.rem(to, NYLO)
        lanes = pl.ds(pl.multiple_of(half * LANES, LANES), LANES)
        for z in range(NZ):
            start = pl.multiple_of((z * NYLO + low) * PER_BLK, 8)
            tail = start + (NYHI * at + half) * TAIL_ROWS
            rows = [
                total[pl.ds(start, PER_BLK), lanes],
                tails[pl.ds(tail, TAIL_ROWS), :],
            ]
            piece[z] = jnp.concatenate(rows, axis=0).astype(BF16)


def add_kernel(*refs):
    parts, out = refs[:-1], refs[-1]
    total = parts[0][...].astype(F32)
    for part in parts[1:]:
        total = total + part[...].astype(F32)
    out[...] = total.astype(BF16)


def add_z_kernel(pieces, out):
    total = pieces[0].astype(F32)
    for place in range(1, NZ):
        total = total + pieces[place].astype(F32)
    out[...] = total.astype(BF16)


def place_kernel(mine, other, out):
    core = lax.axis_index("core")
    at = lax.axis_index("x")
    half_at = lax.axis_index("yhi")
    for step in range(NX):
        came_x = lax.rem(at + NX - step, NX)
        for flip in range(NYHI):
            index = NYHI * came_x + lax.rem(half_at + flip, NYHI)
            own = mine[step, flip]
            across = other[step, flip]
            lanes = pl.ds(pl.multiple_of(index * LANES, LANES), LANES)
            rows = pl.ds(index * TAIL_ROWS, TAIL_ROWS)
            for head, part in enumerate((pick(core, own, across), pick(core, across, own))):
                part = part.astype(F32)
                out[:, head, lanes] = part[:PER_BLK]
                out[rows, head, TAIL_AT:] = part[PER_BLK:]


def z_shift(array, by):
    return lax.ppermute(array, "z", [(z, (z + by) % NZ) for z in range(NZ)])


def u_shift(array):
    pairs = []
    for z in range(NZ):
        pairs.append((z * NYLO, ((z + 1) % NZ) * NYLO))
        pairs.append((z * NYLO + 1, ((z - 1) % NZ) * NYLO + 1))
    return lax.ppermute(array, BLK, pairs)


def y_swap(array):
    return lax.ppermute(array, "ylo", [(0, 1), (1, 0)])


def core_swap(array):
    return lax.ppermute(array, "core", [(0, 1), (1, 0)])


def x_turn(array, by):
    return lax.ppermute(array, "x", [(i, (i + by) % NX) for i in range(NX)])


def y_turn(array, by):
    index = lambda y: (y % NYLO) * NYHI + y // NYLO
    pairs = [(index(y), index((y + by) % NY)) for y in range(NY)]
    return lax.ppermute(array, ("ylo", "yhi"), pairs)


def half_swap(array):
    return lax.ppermute(array, "yhi", [(0, 1), (1, 0)])


def body(image_feats, text_feats, image_head, text_head, log_scale, bias):
    image = image_feats[0]
    text = text_feats[0]
    scalars = jnp.concatenate([log_scale, bias])
    block = shape((ROWS, D))
    block32 = shape((ROWS, D), F32)
    column = shape((ROWS, 1), F32)

    text_1 = z_shift(text, 1)
    image_1 = z_shift(image, -1)
    both, raw_u = call(choose_kernel, "choose", [shape((2, ROWS, D)), block], (image, text))
    raw_v0 = y_swap(raw_u)
    packed = call(pack_feats_kernel, "pack_feats", shape((2, ROWS, D)), (both, core_swap(both)))
    feats_1, feats_3 = x_turn(packed, 1), x_turn(packed, 3)
    image_1, text_1, packed = lax.optimization_barrier((image_1, text_1, packed))
    came = (image_1, text_1, image_head, text_head)
    v1 = call(functools.partial(project_came_kernel, 0), "project_v", block, came)
    u2 = y_swap(v1)
    raw_v0, both, image_1, text_1, v1 = lax.optimization_barrier(
        (raw_v0, both, image_1, text_1, v1)
    )
    came = (image_1, text_1, image_head, text_head)
    u1 = call(functools.partial(project_came_kernel, 1), "project_u", block, came)
    u, v, unit_u, unit_v, norm_u, norm_v, scalars = call(
        project_kernel, "project",
        [block, block, block32, block32, column, column, shape((8, LANES), F32)],
        (scalars, both, image_head, text_head), in_specs=[SMEM_SPEC] + [VMEM_SPEC] * 3,
    )
    grad_u, grad_v = call(
        early_kernel, "early", [block32, block32],
        (scalars, u, v, u1, v1, raw_v0, image_head, text_head),
        scratch=[pltpu.VMEM((ROWS, D), BF16)],
    )
    u2, u1, grad_u, grad_v, feats_1, feats_3 = lax.optimization_barrier(
        (u2, u1, grad_u, grad_v, feats_1, feats_3)
    )
    u3 = u_shift(u2)
    v3 = y_swap(u1)
    feats_2 = (x_turn(feats_1[0], 1), x_turn(feats_3[1], 3))
    grad_v = call(
        middle_kernel, "middle", block32, (scalars, v, u2, grad_v)
    )
    sent = shape((2, SENT, ROWS))
    image_dpre, text_dpre, *parts = call(
        late_kernel, "late", [block, block, sent, sent, sent, sent],
        (scalars, u, v, u3, v3, grad_u, grad_v, unit_u, unit_v, norm_u, norm_v),
        scratch=[pltpu.VMEM((D, ROWS), BF16)] * 2,
    )
    image_dpre, text_dpre, feats_2 = lax.optimization_barrier((image_dpre, text_dpre, feats_2))
    image_out, text_out = call(
        feats_grad_kernel, "feats_grad", [block, block],
        (image_dpre, text_dpre, image_head, text_head),
    )
    feats_own, feats_across = call(
        turn_kernel, "turn", [shape((D, NX * ROWS))] * 2, (packed, feats_1, feats_3, *feats_2)
    )
    far = x_turn(parts[2], 2)
    came = [x_turn(parts[1], 1), x_turn(parts[3], 3), far]
    came, image_out, text_out, feats_own, feats_across = lax.optimization_barrier(
        (came, image_out, text_out, feats_own, feats_across)
    )
    parts = [parts[0]] + came
    others = call(others_kernel, "others", shape((NX, SENT, ROWS)), parts)
    across = core_swap(others)
    own_head = call(
        own_head_kernel, "own_head", shape((D, SENT), F32), [feats_own] + parts,
        scratch=[pltpu.VMEM((SENT, NX * ROWS), BF16)],
    )
    pieces = call(
        head_kernel, "head", [shape((NZ, PIECE, LANES))] * NY, (feats_across, across, own_head),
        scratch=[
            pltpu.VMEM((SENT, NX * ROWS), BF16),
            pltpu.VMEM((D, SENT), F32),
            pltpu.VMEM((D, LANES), F32),
        ],
    )
    pieces = [pieces[0]] + [y_turn(pieces[by], by) for by in (2, 1, 3)]
    pieces = call(add_kernel, "add_y", shape((NZ, PIECE, LANES)), pieces)
    pieces = lax.all_to_all(pieces, "z", 0, 0, tiled=True)
    mine = call(add_z_kernel, "add_z", shape((PIECE, LANES)), (pieces,))
    two = jnp.stack([mine, half_swap(mine)])
    far = x_turn(two, 2)
    eight = jnp.stack([two, x_turn(two, 1), far, x_turn(two, 3)])
    places = (eight, core_swap(eight))
    head_grads = call(place_kernel, "place", shape((PER_BLK, 2, D), F32), places)
    return (image_out[None], text_out[None], head_grads)


def solution(mesh):
    split = Mesh(mesh.devices.reshape(NZ, NYLO, NYHI, NX, NCORE), BLK + REP)
    rows = P(REP, BLK, None)
    return jax.shard_map(
        body,
        mesh=split,
        in_specs=(rows, rows, P(), P(), P(), P()),
        out_specs=(rows, rows, P(BLK, None, None)),
        check_vma=False,
    )
```
